768 devices in a mesh: gz: 96 (over z, x, core), view: 4 (over y_lo), gy: 2 (over y_hi).
Axes of the slice: x: 4, y: 8 (y_hi: 2, y_lo: 4; y = y_hi * 4 + y_lo), z: 12, core: 2. Of those that a mesh axis runs over, the one named last changes fastest.
Arguments:
- estimate: bfloat16 [384, 64, 1024], P('gz', 'gy', 'view'), may hold values from 0.099609375 to 10
- observed: float32 [8, 384, 64, 1024], P('view', 'gz', 'gy'), may hold values from 0.5 to 20
- psf_blocks: bfloat16 [8, 196608], P('view', 'gz'), may hold values from 0.0007972717 to 0.0079956055
- kernel_y: float32 [8, 9], replicated, may hold values from 0.01 to 1
- block_source: int32 [8, 8], replicated, may hold values from 0 to 7, as said below
- psf_columns: int32 [8, 16, 3], replicated, may hold values from 0 to 15, as said below
Outputs:
- ratio: float32 [8, 384, 64, 1024], P('view', 'gz', 'gy')
The draws below stay inside these ranges and needn't reach their ends.
Inputs may be any that keep to these rules, and one draw needn't show every extreme that they name: `block_source`: each view v has an offset o_v and reads, for its block j, either block (o_v + j) mod 8 or block (o_v + j // 2) mod 8. Of the entries of one row, at most 4 name blocks held by one index of view (blocks p * 2 to p * 2 + 1), and in every draw some view reaches 4 for some index. psf_columns[v, i, k] = (i + d) mod 16 with the 3 values d of a row distinct, among -2 to 2.
All inputs are finite; a program needn't handle non-finite values.
Results may differ from the reference program's by a relative error of at most 0.0016.
Values may be sent and summed in bfloat16 or wider, within the bound.
No kernel may reach another device: no remote copies, remote signals or barrier semaphores. Data moves between devices by JAX's collectives and lax.ppermute only.
A program may use at most 32 MiB of HBM per device.

```python
import math
import jax
import jax.numpy as jnp
from jax import lax

VIEWS = 8
BLOCKS_DEV = 2
HALF = 4
BAND = 3
XB = 8
X = 1024
SUBBLOCKS = 16
OPLEN = 196608
Z = 384
Y = 64


def draw_block_source(key, part):
    key = jax.random.fold_in(key, 11)
    first, second, third, fourth = jax.random.split(key, 4)
    offsets = jax.random.randint(first, (VIEWS,), 0, XB)
    magnify = jax.random.randint(second, (VIEWS,), 0, 2)
    forced = jax.random.randint(third, (), 0, VIEWS)
    aligned = jax.random.randint(fourth, (), 0, XB // BLOCKS_DEV) * BLOCKS_DEV
    view_ids = jnp.arange(VIEWS)
    offsets = jnp.where(view_ids == forced, aligned, offsets)
    magnify = jnp.where(view_ids == forced, 1, magnify)
    column = jnp.arange(XB)[None, :]
    stride = jnp.where(magnify[:, None] == 1, column // 2, column)
    return ((offsets[:, None] + stride) % XB).astype(jnp.int32)


def draw_psf_columns(key, part):
    key = jax.random.fold_in(key, 23)
    scores = jax.random.randint(key, (VIEWS, SUBBLOCKS, 5), 0, 1000) * 5 + jnp.arange(5)
    chosen = jax.lax.top_k(scores, BAND)[1]
    rows_ids = jnp.arange(SUBBLOCKS)[None, :, None]
    return ((rows_ids + chosen - 2) % SUBBLOCKS).astype(jnp.int32)


def shard_levels(stream_key, shape, cuts, least, top_value):
    loudness, own = 1.0, jax.random.fold_in(stream_key, 6)
    for dim, parts in cuts:
        draws = jnp.exp(jax.random.uniform(jax.random.fold_in(own, dim), (parts,), jnp.float32, least / len(cuts), top_value / len(cuts)))
        loudness = loudness * jnp.repeat(draws, shape[dim] // parts).reshape([-1 if axis == dim else 1 for axis in range(len(shape))])
    return loudness


def setup_inputs(seed: int = 0) -> dict:
    splits = jax.random.split(jax.random.key(seed), 7)
    return {
        "estimate": jnp.clip(jnp.exp(math.log(10.0) - 4.609084 * jax.random.uniform(splits[0], (Z, Y, X), jnp.float32) ** shard_levels(splits[0], (Z, Y, X), ((0, 96), (1, 2), (2, 4)), -0.2, 0.2)), 0.099609375, 10.0).astype(jnp.bfloat16),
        "observed": jnp.clip(jnp.exp(math.log(20.0) - 3.6888795 * jax.random.uniform(splits[1], (VIEWS, Z, Y, X), jnp.float32) ** shard_levels(splits[1], (VIEWS, Z, Y, X), ((0, 4), (1, 96), (2, 2)), -0.2, 0.2)), 0.5, 20.0),
        "psf_blocks": jnp.clip(jnp.exp(math.log(0.0079956055) - 2.3054518 * jax.random.uniform(splits[2], (VIEWS, OPLEN), jnp.float32) ** shard_levels(splits[2], (VIEWS, OPLEN), ((0, 4), (1, 96)), -0.2, 0.2)), 0.0007972717, 0.0079956055).astype(jnp.bfloat16),
        "kernel_y": jnp.clip(jnp.exp(jax.random.uniform(splits[3], (VIEWS, 2 * HALF + 1), jnp.float32, math.log(0.01), math.log(1.0))), 0.01, 1.0),
        "block_source": draw_block_source(jax.random.fold_in(splits[6], 71), 0),
        "psf_columns": draw_psf_columns(jax.random.fold_in(splits[6], 71), 0),
    }


def lateral_blur(moved, operator_rows, columns):
    rows_total = moved.shape[0]
    picked = jnp.take(moved, columns, axis=1).reshape(rows_total, SUBBLOCKS, BAND * 64)
    matrix = operator_rows.reshape(SUBBLOCKS, BAND * 64, 64)
    return jnp.einsum("rik,iko->rio", picked.astype(jnp.float32), matrix.astype(jnp.float32))


def reference(estimate, observed, psf_blocks, kernel_y, block_source, psf_columns):
    pieces = estimate.reshape(Z, Y, XB, 128)

    def single_view(inputs):
        seen, operator_rows, weights, sources, columns = inputs
        moved = jnp.take(pieces, sources, axis=2).reshape(Z * Y, SUBBLOCKS, 64)
        flat = lateral_blur(moved, operator_rows, columns).reshape(Z, Y, X).astype(jnp.bfloat16)
        flat = lax.optimization_barrier(flat)
        padded = jnp.pad(flat.astype(jnp.float32), ((0, 0), (HALF, HALF), (0, 0)))
        blurred = jnp.zeros((Z, Y, X), jnp.float32)
        for offset in range(2 * HALF + 1):
            blurred = blurred + weights[offset] * padded[:, offset:offset + Y, :]
        return seen / blurred

    return lax.map(single_view, (observed, psf_blocks, kernel_y, block_source, psf_columns))
```

```python
import jax
import jax.numpy as jnp
from jax import lax
from jax.experimental import pallas as pl
from jax.experimental.pallas import tpu as pltpu
from jax.sharding import Mesh, PartitionSpec as P

PLANES, ROWS, HALO = 4, 32, 4
OWN = PLANES * ROWS
EDGE = PLANES * HALO
BLOCKS = 8
BAND = 3


def fused(place, sources, columns, weights, seen, mine, other, observed, ratio, dense, flat):
    view, side, core = place[0], place[1], place[2]
    dense[...] = jnp.zeros_like(dense)
    for w in range(2):
        for i in range(2 * BLOCKS):
            j, half = i // 2, i % 2
            for k in range(BAND):
                shift = (columns[2 * view + w, i * BAND + k] - (2 * j - 2)) & 15
                base = shift * 64
                lanes = pl.ds(64 * half, 64)
                dense[w, j, pl.ds(pl.multiple_of(base + 32 * core, 32), 32), lanes] = mine[
                    i * BAND + k, :, 64 * w : 64 * w + 64
                ]
                dense[w, j, pl.ds(pl.multiple_of(base + 32 * (1 - core), 32), 32), lanes] = other[
                    i * BAND + k, :, 64 * w : 64 * w + 64
                ]

    def block(w, j):
        b = sources[2 * view + w, j % BLOCKS]
        p, half = b // 2, b % 2
        return jnp.concatenate([seen[p, half, :OWN], seen[3 - p, half, OWN:]], axis=0)

    for w in range(2):
        for j in range(BLOCKS):
            near = jnp.concatenate([block(w, j + BLOCKS - 1), block(w, j), block(w, j + 1)], axis=1)
            flat[w, :, 128 * j : 128 * j + 128] = jnp.dot(
                near, dense[w, j], preferred_element_type=jnp.float32
            ).astype(jnp.bfloat16)

    shape = (OWN, OWN + EDGE)
    row = lax.broadcasted_iota(jnp.int32, shape, 0)
    col = lax.broadcasted_iota(jnp.int32, shape, 1)
    outer = col - OWN
    spot = jnp.where(col < OWN, col & (ROWS - 1), (outer & (HALO - 1)) + jnp.where(side == 0, ROWS, -HALO))
    plane = jnp.where(col < OWN, col >> 5, outer >> 2)
    tap = jnp.where(plane == (row >> 5), spot - (row & (ROWS - 1)) + HALO, -1)
    for w in range(2):
        mix = jnp.zeros(shape, jnp.float32)
        for t in range(2 * HALO + 1):
            mix = jnp.where(tap == t, weights[2 * view + w, t], mix)
        high = mix.astype(jnp.bfloat16)
        low = (mix - high.astype(jnp.float32)).astype(jnp.bfloat16)
        lateral = flat[w]
        blurred = jnp.dot(high, lateral, preferred_element_type=jnp.float32)
        blurred = blurred + jnp.dot(low, lateral, preferred_element_type=jnp.float32)
        ratio[w] = observed[w] / blurred


def shards(estimate, observed, psf_blocks, kernel_y, block_source, psf_columns):
    side = lax.axis_index("gy")
    place = jnp.stack([lax.axis_index("view"), side, lax.axis_index("core")]).astype(jnp.int32)
    shard = psf_blocks.reshape(2, 32, 64).transpose(1, 0, 2).reshape(1, 32, 128)
    edge = lax.dynamic_slice_in_dim(estimate, jnp.where(side == 0, ROWS - HALO, 0), HALO, 1)
    mirror = [(v * 2 + g, (3 - v) * 2 + (1 - g)) for v in range(4) for g in range(2)]
    edge = lax.ppermute(edge, ("view", "gy"), mirror)
    across = lax.all_to_all(jnp.broadcast_to(shard, (4, 32, 128)), "x", 0, 0, tiled=True)
    slab = jnp.concatenate([estimate.reshape(OWN, 2, 128), edge.reshape(EDGE, 2, 128)], axis=0)
    slab = slab.transpose(1, 0, 2)
    seen = lax.all_to_all(jnp.broadcast_to(slab[None], (4, *slab.shape)), "view", 0, 0, tiled=True)
    mine = lax.all_to_all(jnp.broadcast_to(across[None], (12, 4, 32, 128)), "z", 0, 0, tiled=True)
    mine = mine.reshape(48, 32, 128)
    other = lax.ppermute(mine, "core", [(0, 1), (1, 0)])
    smem = pl.BlockSpec(memory_space=pltpu.SMEM)
    vmem = pl.BlockSpec(memory_space=pltpu.VMEM)
    ratio = pl.pallas_call(
        fused,
        out_shape=jax.ShapeDtypeStruct((2, OWN, 1024), jnp.float32),
        in_specs=[smem] * 4 + [vmem] * 4,
        out_specs=vmem,
        scratch_shapes=[
            pltpu.VMEM((2, BLOCKS, 384, 128), jnp.bfloat16),
            pltpu.VMEM((2, OWN + EDGE, 1024), jnp.bfloat16),
        ],
        compiler_params=pltpu.CompilerParams(vmem_limit_bytes=32 * 1024 * 1024),
    )(
        place,
        block_source,
        psf_columns.reshape(8, 48),
        kernel_y,
        seen,
        mine,
        other,
        observed.reshape(2, OWN, 1024),
    )
    return ratio.reshape(2, PLANES, ROWS, 1024)


def solution(mesh):
    fine = Mesh(mesh.devices.reshape(12, 4, 2, 4, 2), ("z", "x", "core", "view", "gy"))
    gz = ("z", "x", "core")
    in_specs = (P(gz, "gy", "view"), P("view", gz, "gy", None), P("view", gz), P(), P(), P())
    out_specs = P("view", gz, "gy", None)
    return jax.shard_map(shards, mesh=fine, in_specs=in_specs, out_specs=out_specs, check_vma=False)
```

```python
import jax
import jax.numpy as jnp
from jax import lax
from jax.experimental import pallas as pl
from jax.experimental.pallas import tpu as pltpu
from jax.sharding import Mesh, PartitionSpec as P

PLANES, ROWS, HALO = 4, 32, 4
OWN = PLANES * ROWS
EDGE = PLANES * HALO
BLOCKS = 8
BAND = 3


def fused(place, sources, columns, weights, near, far, mine, other, observed, ratio, dense, flat, seen):
    view, side, core = place[0], place[1], place[2]
    seen[view] = near[0]
    seen[view ^ 1] = near[1]
    seen[view ^ 2] = far[0]
    seen[view ^ 3] = far[1]
    dense[...] = jnp.zeros_like(dense)
    for w in range(2):
        for i in range(2 * BLOCKS):
            j, half = i // 2, i % 2
            for k in range(BAND):
                shift = (columns[2 * view + w, i * BAND + k] - (2 * j - 2)) & 15
                base = shift * 64
                lanes = pl.ds(64 * half, 64)
                dense[w, j, pl.ds(pl.multiple_of(base + 32 * core, 32), 32), lanes] = mine[
                    i * BAND + k, :, 64 * w : 64 * w + 64
                ]
                dense[w, j, pl.ds(pl.multiple_of(base + 32 * (1 - core), 32), 32), lanes] = other[
                    i * BAND + k, :, 64 * w : 64 * w + 64
                ]

    def block(w, j):
        b = sources[2 * view + w, j % BLOCKS]
        p, half = b // 2, b % 2
        return jnp.concatenate([seen[p, half, :OWN], seen[3 - p, half, OWN:]], axis=0)

    for w in range(2):
        for j in range(BLOCKS):
            wide = jnp.concatenate([block(w, j + BLOCKS - 1), block(w, j), block(w, j + 1)], axis=1)
            flat[w, :, 128 * j : 128 * j + 128] = jnp.dot(
                wide, dense[w, j], preferred_element_type=jnp.float32
            ).astype(jnp.bfloat16)

    shape = (OWN, OWN + EDGE)
    row = lax.broadcasted_iota(jnp.int32, shape, 0)
    col = lax.broadcasted_iota(jnp.int32, shape, 1)
    outer = col - OWN
    spot = jnp.where(col < OWN, col & (ROWS - 1), (outer & (HALO - 1)) + jnp.where(side == 0, ROWS, -HALO))
    plane = jnp.where(col < OWN, col >> 5, outer >> 2)
    tap = jnp.where(plane == (row >> 5), spot - (row & (ROWS - 1)) + HALO, -1)
    for w in range(2):
        mix = jnp.zeros(shape, jnp.float32)
        for t in range(2 * HALO + 1):
            mix = jnp.where(tap == t, weights[2 * view + w, t], mix)
        high = mix.astype(jnp.bfloat16)
        low = (mix - high.astype(jnp.float32)).astype(jnp.bfloat16)
        lateral = flat[w]
        blurred = jnp.dot(high, lateral, preferred_element_type=jnp.float32)
        blurred = blurred + jnp.dot(low, lateral, preferred_element_type=jnp.float32)
        ratio[w] = observed[w] / blurred


def shards(estimate, observed, psf_blocks, kernel_y, block_source, psf_columns):
    side = lax.axis_index("gy")
    place = jnp.stack([lax.axis_index("view"), side, lax.axis_index("core")]).astype(jnp.int32)
    shard = psf_blocks.reshape(2, 32, 64).transpose(1, 0, 2).reshape(1, 32, 128)
    edge = lax.dynamic_slice_in_dim(estimate, jnp.where(side == 0, ROWS - HALO, 0), HALO, 1)
    mirror = [(v * 2 + g, (3 - v) * 2 + (1 - g)) for v in range(4) for g in range(2)]
    edge = lax.ppermute(edge, ("view", "gy"), mirror)
    across = lax.all_to_all(jnp.broadcast_to(shard, (4, 32, 128)), "x", 0, 0, tiled=True)
    edge, across = lax.optimization_barrier((edge, across))
    slab = jnp.concatenate([estimate.reshape(OWN, 2, 128), edge.reshape(EDGE, 2, 128)], axis=0)
    slab = slab.transpose(1, 0, 2)[None]
    near = jnp.concatenate([slab, lax.ppermute(slab, "view", [(i, i ^ 1) for i in range(4)])], axis=0)
    far = lax.ppermute(near, "view", [(i, i ^ 2) for i in range(4)])
    mine = lax.all_to_all(jnp.broadcast_to(across[None], (12, 4, 32, 128)), "z", 0, 0, tiled=True)
    mine, far = lax.optimization_barrier((mine.reshape(48, 32, 128), far))
    other = lax.ppermute(mine, "core", [(0, 1), (1, 0)])
    smem = pl.BlockSpec(memory_space=pltpu.SMEM)
    vmem = pl.BlockSpec(memory_space=pltpu.VMEM)
    ratio = pl.pallas_call(
        fused,
        out_shape=jax.ShapeDtypeStruct((2, OWN, 1024), jnp.float32),
        in_specs=[smem] * 4 + [vmem] * 5,
        out_specs=vmem,
        scratch_shapes=[
            pltpu.VMEM((2, BLOCKS, 384, 128), jnp.bfloat16),
            pltpu.VMEM((2, OWN + EDGE, 1024), jnp.bfloat16),
            pltpu.VMEM((4, 2, OWN + EDGE, 128), jnp.bfloat16),
        ],
        compiler_params=pltpu.CompilerParams(vmem_limit_bytes=32 * 1024 * 1024),
    )(
        place,
        block_source,
        psf_columns.reshape(8, 48),
        kernel_y,
        near,
        far,
        mine,
        other,
        observed.reshape(2, OWN, 1024),
    )
    return ratio.reshape(2, PLANES, ROWS, 1024)


def solution(mesh):
    fine = Mesh(mesh.devices.reshape(12, 4, 2, 4, 2), ("z", "x", "core", "view", "gy"))
    gz = ("z", "x", "core")
    in_specs = (P(gz, "gy", "view"), P("view", gz, "gy", None), P("view", gz), P(), P(), P())
    out_specs = P("view", gz, "gy", None)
    return jax.shard_map(shards, mesh=fine, in_specs=in_specs, out_specs=out_specs, check_vma=False)
```

```python
import jax
import jax.numpy as jnp
from jax import lax
from jax.experimental import pallas as pl
from jax.experimental.pallas import tpu as pltpu
from jax.sharding import Mesh, PartitionSpec as P

PLANES, ROWS, HALO = 4, 32, 4
OWN = PLANES * ROWS
EDGE = PLANES * HALO
BLOCKS = 8
BAND = 3


def fused(place, sources, columns, weights, own, one, two, three, edge, mine, other, observed, ratio, dense, flat, seen):
    view, side, core = place[0], place[1], place[2]
    for k, part in enumerate((own, one, two, three)):
        seen[view ^ k, :, :OWN] = part[...]
        seen[view ^ 3 ^ k, :, OWN:] = edge[k]
    dense[...] = jnp.zeros_like(dense)
    for w in range(2):
        for i in range(2 * BLOCKS):
            j, half = i // 2, i % 2
            for k in range(BAND):
                shift = (columns[2 * view + w, i * BAND + k] - (2 * j - 2)) & 15
                base = shift * 64
                lanes = pl.ds(64 * half, 64)
                q = i * BAND + k
                s = q % 4 * 12 + q // 4
                dense[w, j, pl.ds(pl.multiple_of(base + 32 * core, 32), 32), lanes] = mine[
                    s, :, 64 * w : 64 * w + 64
                ]
                dense[w, j, pl.ds(pl.multiple_of(base + 32 * (1 - core), 32), 32), lanes] = other[
                    s, :, 64 * w : 64 * w + 64
                ]

    def block(w, j):
        b = sources[2 * view + w, j % BLOCKS]
        p, half = b // 2, b % 2
        return seen[p, half]

    for w in range(2):
        for j in range(BLOCKS):
            wide = jnp.concatenate([block(w, j + BLOCKS - 1), block(w, j), block(w, j + 1)], axis=1)
            flat[w, :, 128 * j : 128 * j + 128] = jnp.dot(
                wide, dense[w, j], preferred_element_type=jnp.float32
            ).astype(jnp.bfloat16)

    shape = (OWN, OWN + EDGE)
    row = lax.broadcasted_iota(jnp.int32, shape, 0)
    col = lax.broadcasted_iota(jnp.int32, shape, 1)
    outer = col - OWN
    spot = jnp.where(col < OWN, col & (ROWS - 1), (outer & (HALO - 1)) + jnp.where(side == 0, ROWS, -HALO))
    plane = jnp.where(col < OWN, col >> 5, outer >> 2)
    tap = jnp.where(plane == (row >> 5), spot - (row & (ROWS - 1)) + HALO, -1)
    for w in range(2):
        mix = jnp.zeros(shape, jnp.float32)
        for t in range(2 * HALO + 1):
            mix = jnp.where(tap == t, weights[2 * view + w, t], mix)
        high = mix.astype(jnp.bfloat16)
        low = (mix - high.astype(jnp.float32)).astype(jnp.bfloat16)
        lateral = flat[w]
        blurred = jnp.dot(high, lateral, preferred_element_type=jnp.float32)
        blurred = blurred + jnp.dot(low, lateral, preferred_element_type=jnp.float32)
        ratio[w] = observed[w] / blurred


def shards(estimate, observed, psf_blocks, kernel_y, block_source, psf_columns):
    side = lax.axis_index("gy")
    place = jnp.stack([lax.axis_index("view"), side, lax.axis_index("core")]).astype(jnp.int32)
    shard = psf_blocks.reshape(2, 32, 64).transpose(1, 0, 2).reshape(1, 32, 128)
    along = lax.all_to_all(jnp.broadcast_to(shard, (12, 32, 128)), "z", 0, 0, tiled=True)
    slab = estimate.reshape(PLANES, ROWS, 2, 128).transpose(2, 0, 1, 3)
    parts = [lax.ppermute(slab, "view", [(i, i ^ k) for i in range(4)]) for k in (1, 2, 3)]
    along, *parts = lax.optimization_barrier((along, *parts))
    mine = lax.all_to_all(jnp.broadcast_to(along[None], (4, 12, 32, 128)), "x", 0, 0, tiled=True)
    begin = jnp.where(side == 0, ROWS - HALO, 0)
    edge = jnp.stack([lax.dynamic_slice_in_dim(part, begin, HALO, 2) for part in (slab, *parts)])
    mirror = [(v * 2 + g, (3 - v) * 2 + (1 - g)) for v in range(4) for g in range(2)]
    edge = lax.ppermute(edge, ("view", "gy"), mirror).reshape(4, 2, EDGE, 128)
    mine, edge = lax.optimization_barrier((mine.reshape(48, 32, 128), edge))
    other = lax.ppermute(mine, "core", [(0, 1), (1, 0)])
    smem = pl.BlockSpec(memory_space=pltpu.SMEM)
    vmem = pl.BlockSpec(memory_space=pltpu.VMEM)
    ratio = pl.pallas_call(
        fused,
        out_shape=jax.ShapeDtypeStruct((2, OWN, 1024), jnp.float32),
        in_specs=[smem] * 4 + [vmem] * 8,
        out_specs=vmem,
        scratch_shapes=[
            pltpu.VMEM((2, BLOCKS, 384, 128), jnp.bfloat16),
            pltpu.VMEM((2, OWN + EDGE, 1024), jnp.bfloat16),
            pltpu.VMEM((4, 2, OWN + EDGE, 128), jnp.bfloat16),
        ],
        compiler_params=pltpu.CompilerParams(vmem_limit_bytes=32 * 1024 * 1024),
    )(
        place,
        block_source,
        psf_columns.reshape(8, 48),
        kernel_y,
        *[part.reshape(2, OWN, 128) for part in (slab, *parts)],
        edge,
        mine,
        other,
        observed.reshape(2, OWN, 1024),
    )
    return ratio.reshape(2, PLANES, ROWS, 1024)


def solution(mesh):
    fine = Mesh(mesh.devices.reshape(12, 4, 2, 4, 2), ("z", "x", "core", "view", "gy"))
    gz = ("z", "x", "core")
    in_specs = (P(gz, "gy", "view"), P("view", gz, "gy", None), P("view", gz), P(), P(), P())
    out_specs = P("view", gz, "gy", None)
    return jax.shard_map(shards, mesh=fine, in_specs=in_specs, out_specs=out_specs, check_vma=False)
```

```python
import jax
import jax.numpy as jnp
from jax import lax
from jax.experimental import pallas as pl
from jax.experimental.pallas import tpu as pltpu
from jax.sharding import Mesh, PartitionSpec as P

PLANES, ROWS, HALO = 4, 32, 4
OWN = PLANES * ROWS
EDGE = PLANES * HALO
BLOCKS = 8
BAND = 3
AHEAD = 4


def fused(place, numbers, weights, own, one, two, three, edge, mine, other, observed, ratio, dense, flat, seen):
    view, side, core = place[0], place[1], place[2]
    for k, part in enumerate((own, one, two, three)):
        seen[view ^ k, :, :OWN] = part[...]
        seen[view ^ 3 ^ k, :, OWN:] = edge[k]
    dense[...] = jnp.zeros_like(dense)
    for w in range(2):
        for i in range(2 * BLOCKS):
            j, half = i // 2, i % 2
            for k in range(BAND):
                shift = (numbers[w, BLOCKS + i * BAND + k] - (2 * j - 2)) & 15
                base = shift * 64
                lanes = pl.ds(64 * half, 64)
                q = i * BAND + k
                s = q % 4 * 12 + q // 4
                dense[w, j, pl.ds(pl.multiple_of(base + 32 * core, 32), 32), lanes] = mine[
                    s, :, 64 * w : 64 * w + 64
                ]
                dense[w, j, pl.ds(pl.multiple_of(base + 32 * (1 - core), 32), 32), lanes] = other[
                    s, :, 64 * w : 64 * w + 64
                ]

    def block(w, j):
        b = numbers[w, j % BLOCKS]
        p, half = b // 2, b % 2
        return seen[p, half]

    for w in range(2):
        for j in range(BLOCKS):
            wide = jnp.concatenate([block(w, j + BLOCKS - 1), block(w, j), block(w, j + 1)], axis=1)
            flat[w, :, 128 * j : 128 * j + 128] = jnp.dot(
                wide, dense[w, j], preferred_element_type=jnp.float32
            ).astype(jnp.bfloat16)

    shape = (OWN, OWN + EDGE)
    row = lax.broadcasted_iota(jnp.int32, shape, 0)
    col = lax.broadcasted_iota(jnp.int32, shape, 1)
    outer = col - OWN
    spot = jnp.where(col < OWN, col & (ROWS - 1), (outer & (HALO - 1)) + jnp.where(side == 0, ROWS, -HALO))
    plane = jnp.where(col < OWN, col >> 5, outer >> 2)
    tap = jnp.where(plane == (row >> 5), spot - (row & (ROWS - 1)) + HALO, -1)
    for w in range(2):
        mix = jnp.zeros(shape, jnp.float32)
        for t in range(2 * HALO + 1):
            mix = jnp.where(tap == t, weights[w, t], mix)
        high = mix.astype(jnp.bfloat16)
        low = (mix - high.astype(jnp.float32)).astype(jnp.bfloat16)
        lateral = flat[w]
        blurred = jnp.dot(high, lateral, preferred_element_type=jnp.float32)
        blurred = blurred + jnp.dot(low, lateral, preferred_element_type=jnp.float32)
        ratio[w] = observed[w] / blurred


def swap(array, k, planes):
    return lax.ppermute(array, ("z", "view"), [(4 * z + v, 4 * z + (v ^ k)) for z in planes for v in range(4)])


def shards(estimate, observed, psf_blocks, kernel_y, block_source, psf_columns):
    side = lax.axis_index("gy")
    place = jnp.stack([lax.axis_index("view"), side, lax.axis_index("core")]).astype(jnp.int32)
    shard = psf_blocks.reshape(2, 32, 64).transpose(1, 0, 2).reshape(1, 32, 128)
    slab = estimate.reshape(PLANES, ROWS, 2, 128).transpose(2, 0, 1, 3)
    spread = jnp.broadcast_to(shard, (12, 32, 128))
    ahead = swap(slab, 2, range(AHEAD))
    ahead, spread, estimate = lax.optimization_barrier((ahead, spread, estimate))
    slab = estimate.reshape(PLANES, ROWS, 2, 128).transpose(2, 0, 1, 3)
    along = lax.all_to_all(spread, "z", 0, 0, tiled=True)
    parts = [swap(slab, 1, range(12)), swap(slab, 2, range(AHEAD, 12)), swap(slab, 3, range(12))]
    along, slab, *parts = lax.optimization_barrier((along, slab, *parts))
    parts[1] = jnp.where(lax.axis_index("z") < AHEAD, ahead, parts[1])
    mine = lax.all_to_all(jnp.broadcast_to(along[None], (4, 12, 32, 128)), "x", 0, 0, tiled=True)
    begin = jnp.where(side == 0, ROWS - HALO, 0)
    edge = jnp.stack([lax.dynamic_slice_in_dim(part, begin, HALO, 2) for part in (slab, *parts)])
    mirror = [(v * 2 + g, (3 - v) * 2 + (1 - g)) for v in range(4) for g in range(2)]
    edge = lax.ppermute(edge, ("view", "gy"), mirror).reshape(4, 2, EDGE, 128)
    mine, edge, kernel_y, block_source, psf_columns = lax.optimization_barrier(
        (mine.reshape(48, 32, 128), edge, kernel_y, block_source, psf_columns)
    )
    first = 2 * lax.axis_index("view")
    numbers = jnp.concatenate([block_source, psf_columns.reshape(8, 48)], axis=1)
    numbers = lax.dynamic_slice_in_dim(numbers, first, 2, 0)
    weights = lax.dynamic_slice_in_dim(kernel_y, first, 2, 0)
    other = lax.ppermute(mine, "core", [(0, 1), (1, 0)])
    smem = pl.BlockSpec(memory_space=pltpu.SMEM)
    vmem = pl.BlockSpec(memory_space=pltpu.VMEM)
    ratio = pl.pallas_call(
        fused,
        out_shape=jax.ShapeDtypeStruct((2, OWN, 1024), jnp.float32),
        in_specs=[smem] * 3 + [vmem] * 8,
        out_specs=vmem,
        scratch_shapes=[
            pltpu.VMEM((2, BLOCKS, 384, 128), jnp.bfloat16),
            pltpu.VMEM((2, OWN + EDGE, 1024), jnp.bfloat16),
            pltpu.VMEM((4, 2, OWN + EDGE, 128), jnp.bfloat16),
        ],
        compiler_params=pltpu.CompilerParams(vmem_limit_bytes=32 * 1024 * 1024),
    )(
        place,
        numbers,
        weights,
        *[part.reshape(2, OWN, 128) for part in (slab, *parts)],
        edge,
        mine,
        other,
        observed.reshape(2, OWN, 1024),
    )
    return ratio.reshape(2, PLANES, ROWS, 1024)


def solution(mesh):
    fine = Mesh(mesh.devices.reshape(12, 4, 2, 4, 2), ("z", "x", "core", "view", "gy"))
    gz = ("z", "x", "core")
    in_specs = (P(gz, "gy", "view"), P("view", gz, "gy", None), P("view", gz), P(), P(), P())
    out_specs = P("view", gz, "gy", None)
    return jax.shard_map(shards, mesh=fine, in_specs=in_specs, out_specs=out_specs, check_vma=False)
```

```python
import functools
import itertools

import jax
import jax.numpy as jnp
from jax import lax
from jax.experimental import pallas as pl
from jax.experimental.pallas import tpu as pltpu
from jax.sharding import Mesh, PartitionSpec as P

PLANES, ROWS, HALO = 4, 32, 4
OWN = PLANES * ROWS
EDGE = PLANES * HALO
BLOCKS = 8
BAND = 3
AHEAD = {2: 4, 3: 2}
AXES = ("z", "x", "core", "view", "gy")
SIZES = (12, 4, 2, 4, 2)


def fused(place, numbers, weights, own, one, two, three, edge, mine, other, observed, ratio, dense, flat, seen):
    view, side, core = place[0], place[1], place[2]
    for k, part in enumerate((own, one, two, three)):
        seen[view ^ k, :, :OWN] = part[...]
        seen[view ^ 3 ^ k, :, OWN:] = edge[k]
    dense[...] = jnp.zeros_like(dense)
    for w in range(2):
        for i in range(2 * BLOCKS):
            j, half = i // 2, i % 2
            for k in range(BAND):
                shift = (numbers[w, BLOCKS + i * BAND + k] - (2 * j - 2)) & 15
                base = shift * 64
                lanes = pl.ds(64 * half, 64)
                q = i * BAND + k
                s = q % 4 * 12 + q // 4
                dense[w, j, pl.ds(pl.multiple_of(base + 32 * core, 32), 32), lanes] = mine[
                    s, :, 64 * w : 64 * w + 64
                ]
                dense[w, j, pl.ds(pl.multiple_of(base + 32 * (1 - core), 32), 32), lanes] = other[
                    s, :, 64 * w : 64 * w + 64
                ]

    def block(w, j):
        b = numbers[w, j % BLOCKS]
        p, half = b // 2, b % 2
        return seen[p, half]

    for w in range(2):
        for j in range(BLOCKS):
            wide = jnp.concatenate([block(w, j + BLOCKS - 1), block(w, j), block(w, j + 1)], axis=1)
            flat[w, :, 128 * j : 128 * j + 128] = jnp.dot(
                wide, dense[w, j], preferred_element_type=jnp.float32
            ).astype(jnp.bfloat16)

    shape = (OWN, OWN + EDGE)
    row = lax.broadcasted_iota(jnp.int32, shape, 0)
    col = lax.broadcasted_iota(jnp.int32, shape, 1)
    outer = col - OWN
    spot = jnp.where(col < OWN, col & (ROWS - 1), (outer & (HALO - 1)) + jnp.where(side == 0, ROWS, -HALO))
    plane = jnp.where(col < OWN, col >> 5, outer >> 2)
    tap = jnp.where(plane == (row >> 5), spot - (row & (ROWS - 1)) + HALO, -1)
    for w in range(2):
        mix = jnp.zeros(shape, jnp.float32)
        for t in range(2 * HALO + 1):
            mix = jnp.where(tap == t, weights[w, t], mix)
        high = mix.astype(jnp.bfloat16)
        low = (mix - high.astype(jnp.float32)).astype(jnp.bfloat16)
        lateral = flat[w]
        blurred = jnp.dot(high, lateral, preferred_element_type=jnp.float32)
        blurred = blurred + jnp.dot(low, lateral, preferred_element_type=jnp.float32)
        ratio[w] = observed[w] / blurred


def early(k, z, x, core, gy):
    return (z < AHEAD.get(k, 0)) & ((z + x + core + gy) > 0)


def swap(array, k, chosen):
    pairs = []
    for z, x, core, v, gy in itertools.product(*map(range, SIZES)):
        if chosen(z, x, core, gy):
            place = ((z * SIZES[1] + x) * SIZES[2] + core) * SIZES[3]
            pairs.append(((place + v) * SIZES[4] + gy, (place + (v ^ k)) * SIZES[4] + gy))
    return lax.ppermute(array, AXES, pairs)


def shards(estimate, observed, psf_blocks, kernel_y, block_source, psf_columns):
    side = lax.axis_index("gy")
    place = jnp.stack([lax.axis_index("view"), side, lax.axis_index("core")]).astype(jnp.int32)
    shard = psf_blocks.reshape(2, 32, 64).transpose(1, 0, 2).reshape(1, 32, 128)
    slab = estimate.reshape(PLANES, ROWS, 2, 128).transpose(2, 0, 1, 3)
    spread = jnp.broadcast_to(shard, (12, 32, 128))
    ahead = [swap(slab, k, functools.partial(early, k)) for k in (2, 3)]
    *ahead, spread, estimate = lax.optimization_barrier((*ahead, spread, estimate))
    slab = estimate.reshape(PLANES, ROWS, 2, 128).transpose(2, 0, 1, 3)
    along = lax.all_to_all(spread, "z", 0, 0, tiled=True)
    parts = [swap(slab, k, lambda *at, k=k: not early(k, *at)) for k in (1, 2, 3)]
    along, slab, *parts = lax.optimization_barrier((along, slab, *parts))
    for k in (2, 3):
        here = early(k, *(lax.axis_index(name) for name in ("z", "x", "core", "gy")))
        parts[k - 1] = jnp.where(here, ahead[k - 2], parts[k - 1])
    mine = lax.all_to_all(jnp.broadcast_to(along[None], (4, 12, 32, 128)), "x", 0, 0, tiled=True)
    begin = jnp.where(side == 0, ROWS - HALO, 0)
    edge = jnp.stack([lax.dynamic_slice_in_dim(part, begin, HALO, 2) for part in (slab, *parts)])
    mirror = [(v * 2 + g, (3 - v) * 2 + (1 - g)) for v in range(4) for g in range(2)]
    edge = lax.ppermute(edge, ("view", "gy"), mirror).reshape(4, 2, EDGE, 128)
    mine, edge, kernel_y, block_source, psf_columns = lax.optimization_barrier(
        (mine.reshape(48, 32, 128), edge, kernel_y, block_source, psf_columns)
    )
    first = 2 * lax.axis_index("view")
    numbers = jnp.concatenate([block_source, psf_columns.reshape(8, 48)], axis=1)
    numbers = lax.dynamic_slice_in_dim(numbers, first, 2, 0)
    weights = lax.dynamic_slice_in_dim(kernel_y, first, 2, 0)
    other = lax.ppermute(mine, "core", [(0, 1), (1, 0)])
    smem = pl.BlockSpec(memory_space=pltpu.SMEM)
    vmem = pl.BlockSpec(memory_space=pltpu.VMEM)
    ratio = pl.pallas_call(
        fused,
        out_shape=jax.ShapeDtypeStruct((2, OWN, 1024), jnp.float32),
        in_specs=[smem] * 3 + [vmem] * 8,
        out_specs=vmem,
        scratch_shapes=[
            pltpu.VMEM((2, BLOCKS, 384, 128), jnp.bfloat16),
            pltpu.VMEM((2, OWN + EDGE, 1024), jnp.bfloat16),
            pltpu.VMEM((4, 2, OWN + EDGE, 128), jnp.bfloat16),
        ],
        compiler_params=pltpu.CompilerParams(vmem_limit_bytes=32 * 1024 * 1024),
    )(
        place,
        numbers,
        weights,
        *[part.reshape(2, OWN, 128) for part in (slab, *parts)],
        edge,
        mine,
        other,
        observed.reshape(2, OWN, 1024),
    )
    return ratio.reshape(2, PLANES, ROWS, 1024)


def solution(mesh):
    fine = Mesh(mesh.devices.reshape(SIZES), AXES)
    gz = ("z", "x", "core")
    in_specs = (P(gz, "gy", "view"), P("view", gz, "gy", None), P("view", gz), P(), P(), P())
    out_specs = P("view", gz, "gy", None)
    return jax.shard_map(shards, mesh=fine, in_specs=in_specs, out_specs=out_specs, check_vma=False)
```

```python
import itertools

import jax
import jax.numpy as jnp
from jax import lax
from jax.experimental import pallas as pl
from jax.experimental.pallas import tpu as pltpu
from jax.sharding import Mesh, PartitionSpec as P

PLANES, ROWS, HALO = 4, 32, 4
OWN = PLANES * ROWS
EDGE = PLANES * HALO
BLOCKS = 8
BAND = 3
AHEAD = 5
AXES = ("z", "x", "core", "view", "gy")
SIZES = (12, 4, 2, 4, 2)


def fused(place, numbers, weights, near, far, edge, mine, other, observed, ratio, dense, flat, seen):
    view, side, core = place[0], place[1], place[2]
    parts = (near.at[0], near.at[1], far.at[0], far.at[1])
    for n, k in enumerate((0, 2, 1, 3)):
        seen[view ^ k, :, :OWN] = parts[n][:, :OWN]
        seen[view ^ k ^ 3, :, OWN:] = jnp.where(place[3] == 1, parts[n][:, OWN:], edge[n])
    dense[...] = jnp.zeros_like(dense)
    for w in range(2):
        for i in range(2 * BLOCKS):
            j, half = i // 2, i % 2
            for k in range(BAND):
                shift = (numbers[w, BLOCKS + i * BAND + k] - (2 * j - 2)) & 15
                base = shift * 64
                lanes = pl.ds(64 * half, 64)
                q = i * BAND + k
                s = q % 4 * 12 + q // 4
                dense[w, j, pl.ds(pl.multiple_of(base + 32 * core, 32), 32), lanes] = mine[
                    s, :, 64 * w : 64 * w + 64
                ]
                dense[w, j, pl.ds(pl.multiple_of(base + 32 * (1 - core), 32), 32), lanes] = other[
                    s, :, 64 * w : 64 * w + 64
                ]

    def block(w, j):
        b = numbers[w, j % BLOCKS]
        return seen[b // 2, b % 2]

    for w in range(2):
        for j in range(BLOCKS):
            wide = jnp.concatenate([block(w, j + BLOCKS - 1), block(w, j), block(w, j + 1)], axis=1)
            flat[w, :, 128 * j : 128 * j + 128] = jnp.dot(
                wide, dense[w, j], preferred_element_type=jnp.float32
            ).astype(jnp.bfloat16)

    shape = (OWN, OWN + EDGE)
    row = lax.broadcasted_iota(jnp.int32, shape, 0)
    col = lax.broadcasted_iota(jnp.int32, shape, 1)
    outer = col - OWN
    spot = jnp.where(col < OWN, col & (ROWS - 1), (outer & (HALO - 1)) + jnp.where(side == 0, ROWS, -HALO))
    plane = jnp.where(col < OWN, col >> 5, outer >> 2)
    tap = jnp.where(plane == (row >> 5), spot - (row & (ROWS - 1)) + HALO, -1)
    for w in range(2):
        mix = jnp.zeros(shape, jnp.float32)
        for t in range(2 * HALO + 1):
            mix = jnp.where(tap == t, weights[w, t], mix)
        high = mix.astype(jnp.bfloat16)
        low = (mix - high.astype(jnp.float32)).astype(jnp.bfloat16)
        lateral = flat[w]
        blurred = jnp.dot(high, lateral, preferred_element_type=jnp.float32)
        blurred = blurred + jnp.dot(low, lateral, preferred_element_type=jnp.float32)
        ratio[w] = observed[w] / blurred


def early(z, x, core):
    return (z < AHEAD) & ((z + x + core) > 0)


def permute(array, route, chosen=lambda *at: True):
    pairs = []
    for z, x, core, v, gy in itertools.product(*map(range, SIZES)):
        if chosen(z, x, core):
            to, across = route(v, gy)
            base = ((z * SIZES[1] + x) * SIZES[2] + core) * SIZES[3]
            pairs.append(((base + v) * SIZES[4] + gy, (base + to) * SIZES[4] + across))
    return lax.ppermute(array, AXES, pairs)


def mirror(v, gy):
    return 3 - v, 1 - gy


def shards(estimate, observed, psf_blocks, kernel_y, block_source, psf_columns):
    side = lax.axis_index("gy")
    place = [lax.axis_index("view"), side, lax.axis_index("core"), early(*map(lax.axis_index, AXES[:3]))]
    place = jnp.stack([jnp.asarray(entry, jnp.int32) for entry in place])
    shard = psf_blocks.reshape(2, 32, 64).transpose(1, 0, 2).reshape(1, 32, 128)
    spread = jnp.broadcast_to(shard, (12, 32, 128))
    begin = jnp.where(side == 0, ROWS - HALO, 0)
    ahead = permute(lax.dynamic_slice_in_dim(estimate, begin, HALO, 1), mirror, early)
    ahead, spread, estimate = lax.optimization_barrier((ahead, spread, estimate))
    along = lax.all_to_all(spread, "z", 0, 0, tiled=True)
    slab = jnp.concatenate([estimate.reshape(OWN, 2, 128), ahead.reshape(EDGE, 2, 128)], axis=0)
    slab = slab.transpose(1, 0, 2)
    two = permute(slab, lambda v, gy: (v ^ 2, gy))
    along, near = lax.optimization_barrier((along, jnp.stack([slab, two])))
    mine = lax.all_to_all(jnp.broadcast_to(along[None], (4, 12, 32, 128)), "x", 0, 0, tiled=True)
    far = permute(near, lambda v, gy: (v ^ 1, gy))
    near, far = lax.optimization_barrier((near, far))
    rows = [part.reshape(2, 2, 18, 8, 128) for part in (near, far)]
    upper = jnp.concatenate([part[:, :, 0:16:4, :HALO] for part in rows])
    lower = jnp.concatenate([part[:, :, 3:16:4, HALO:] for part in rows])
    rows = jnp.where(side == 0, lower, upper)
    edge = permute(rows, mirror, lambda *at: not early(*at)).reshape(4, 2, EDGE, 128)
    mine, edge, kernel_y, block_source, psf_columns = lax.optimization_barrier(
        (mine.reshape(48, 32, 128), edge, kernel_y, block_source, psf_columns)
    )
    first = 2 * lax.axis_index("view")
    numbers = jnp.concatenate([block_source, psf_columns.reshape(8, 48)], axis=1)
    numbers = lax.dynamic_slice_in_dim(numbers, first, 2, 0)
    weights = lax.dynamic_slice_in_dim(kernel_y, first, 2, 0)
    other = lax.ppermute(mine, "core", [(0, 1), (1, 0)])
    smem = pl.BlockSpec(memory_space=pltpu.SMEM)
    vmem = pl.BlockSpec(memory_space=pltpu.VMEM)
    ratio = pl.pallas_call(
        fused,
        out_shape=jax.ShapeDtypeStruct((2, OWN, 1024), jnp.float32),
        in_specs=[smem] * 3 + [vmem] * 6,
        out_specs=vmem,
        scratch_shapes=[
            pltpu.VMEM((2, BLOCKS, 384, 128), jnp.bfloat16),
            pltpu.VMEM((2, OWN + EDGE, 1024), jnp.bfloat16),
            pltpu.VMEM((4, 2, OWN + EDGE, 128), jnp.bfloat16),
        ],
        compiler_params=pltpu.CompilerParams(vmem_limit_bytes=16 * 1024 * 1024),
    )(
        place,
        numbers,
        weights,
        near,
        far,
        edge,
        mine,
        other,
        observed.reshape(2, OWN, 1024),
    )
    return ratio.reshape(2, PLANES, ROWS, 1024)


def solution(mesh):
    fine = Mesh(mesh.devices.reshape(SIZES), AXES)
    gz = ("z", "x", "core")
    in_specs = (P(gz, "gy", "view"), P("view", gz, "gy", None), P("view", gz), P(), P(), P())
    out_specs = P("view", gz, "gy", None)
    return jax.shard_map(shards, mesh=fine, in_specs=in_specs, out_specs=out_specs, check_vma=False)
```

```python
import itertools

import jax
import jax.numpy as jnp
from jax import lax
from jax.experimental import pallas as pl
from jax.experimental.pallas import tpu as pltpu
from jax.sharding import Mesh, PartitionSpec as P

PLANES, ROWS, HALO = 4, 32, 4
OWN = PLANES * ROWS
EDGE = PLANES * HALO
BLOCKS = 8
BAND = 3
AHEAD = 5
AXES = ("z", "x", "core", "view", "gy")
SIZES = (12, 4, 2, 4, 2)


def fused(place, numbers, weights, near, far, edge, mine, other, observed, ratio, dense, flat, seen):
    view, side, core = place[0], place[1], place[2]
    parts = (near.at[0], near.at[1], far.at[0], far.at[1])
    for n, k in enumerate((0, 2, 1, 3)):
        seen[view ^ k, :, :OWN] = parts[n][:, :OWN]
        seen[view ^ k ^ 3, :, OWN:] = jnp.where(place[3] == 1, parts[n][:, OWN:], edge[n])
    dense[...] = jnp.zeros_like(dense)
    for w in range(2):
        for i in range(2 * BLOCKS):
            j, half = i // 2, i % 2
            for k in range(BAND):
                shift = (numbers[w, BLOCKS + i * BAND + k] - (2 * j - 2)) & 15
                base = shift * 64
                lanes = pl.ds(64 * half, 64)
                q = i * BAND + k
                s = q % 4 * 12 + q // 4
                dense[w, j, pl.ds(pl.multiple_of(base + 32 * core, 32), 32), lanes] = mine[
                    s, :, 64 * w : 64 * w + 64
                ]
                dense[w, j, pl.ds(pl.multiple_of(base + 32 * (1 - core), 32), 32), lanes] = other[
                    s, :, 64 * w : 64 * w + 64
                ]

    def block(w, j):
        b = numbers[w, j % BLOCKS]
        return seen[b // 2, b % 2]

    for w in range(2):
        for j in range(BLOCKS):
            wide = jnp.concatenate([block(w, j + BLOCKS - 1), block(w, j), block(w, j + 1)], axis=1)
            flat[w, :, 128 * j : 128 * j + 128] = jnp.dot(
                wide, dense[w, j], preferred_element_type=jnp.float32
            ).astype(jnp.bfloat16)

    shape = (OWN, OWN + EDGE)
    row = lax.broadcasted_iota(jnp.int32, shape, 0)
    col = lax.broadcasted_iota(jnp.int32, shape, 1)
    outer = col - OWN
    spot = jnp.where(col < OWN, col & (ROWS - 1), (outer & (HALO - 1)) + jnp.where(side == 0, ROWS, -HALO))
    plane = jnp.where(col < OWN, col >> 5, outer >> 2)
    tap = jnp.where(plane == (row >> 5), spot - (row & (ROWS - 1)) + HALO, -1)
    for w in range(2):
        mix = jnp.zeros(shape, jnp.float32)
        for t in range(2 * HALO + 1):
            mix = jnp.where(tap == t, weights[w, t], mix)
        high = mix.astype(jnp.bfloat16)
        low = (mix - high.astype(jnp.float32)).astype(jnp.bfloat16)
        lateral = flat[w]
        blurred = jnp.dot(high, lateral, preferred_element_type=jnp.float32)
        blurred = blurred + jnp.dot(low, lateral, preferred_element_type=jnp.float32)
        ratio[w] = observed[w] / blurred


def early(z):
    return z < AHEAD


def permute(array, route, chosen=lambda z: True):
    pairs = []
    for z, x, core, v, gy in itertools.product(*map(range, SIZES)):
        if chosen(z):
            to, across = route(v, gy)
            base = ((z * SIZES[1] + x) * SIZES[2] + core) * SIZES[3]
            pairs.append(((base + v) * SIZES[4] + gy, (base + to) * SIZES[4] + across))
    return lax.ppermute(array, AXES, pairs)


def mirror(v, gy):
    return 3 - v, 1 - gy


def shards(estimate, observed, psf_blocks, kernel_y, block_source, psf_columns):
    side = lax.axis_index("gy")
    place = [lax.axis_index("view"), side, lax.axis_index("core"), early(lax.axis_index("z"))]
    place = jnp.stack([jnp.asarray(entry, jnp.int32) for entry in place])
    shard = psf_blocks.reshape(2, 32, 64).transpose(1, 0, 2).reshape(1, 32, 128)
    spread = jnp.broadcast_to(shard, (12, 32, 128))
    begin = jnp.where(side == 0, ROWS - HALO, 0)
    ahead = permute(lax.dynamic_slice_in_dim(estimate, begin, HALO, 1), mirror, early)
    ahead, spread, estimate = lax.optimization_barrier((ahead, spread, estimate))
    along = lax.all_to_all(spread, "z", 0, 0, tiled=True)
    slab = jnp.concatenate([estimate.reshape(OWN, 2, 128), ahead.reshape(EDGE, 2, 128)], axis=0)
    slab = slab.transpose(1, 0, 2)
    two = permute(slab, lambda v, gy: (v ^ 2, gy))
    along, near = lax.optimization_barrier((along, jnp.stack([slab, two])))
    mine = lax.all_to_all(jnp.broadcast_to(along[None], (4, 12, 32, 128)), "x", 0, 0, tiled=True)
    far = permute(near, lambda v, gy: (v ^ 1, gy))
    mine, near, far = lax.optimization_barrier((mine, near, far))
    rows = [part.reshape(2, 2, 18, 8, 128) for part in (near, far)]
    upper = jnp.concatenate([part[:, :, 0:16:4, :HALO] for part in rows])
    lower = jnp.concatenate([part[:, :, 3:16:4, HALO:] for part in rows])
    rows = jnp.where(side == 0, lower, upper)
    edge = permute(rows, mirror, lambda z: not early(z)).reshape(4, 2, EDGE, 128)
    mine = mine.reshape(48, 32, 128)
    kernel_y, block_source, psf_columns = lax.optimization_barrier(
        (kernel_y, block_source, psf_columns, mine)
    )[:3]
    first = 2 * lax.axis_index("view")
    numbers = jnp.concatenate([block_source, psf_columns.reshape(8, 48)], axis=1)
    numbers = lax.dynamic_slice_in_dim(numbers, first, 2, 0)
    weights = lax.dynamic_slice_in_dim(kernel_y, first, 2, 0)
    other = lax.ppermute(mine, "core", [(0, 1), (1, 0)])
    smem = pl.BlockSpec(memory_space=pltpu.SMEM)
    vmem = pl.BlockSpec(memory_space=pltpu.VMEM)
    ratio = pl.pallas_call(
        fused,
        out_shape=jax.ShapeDtypeStruct((2, OWN, 1024), jnp.float32),
        in_specs=[smem] * 3 + [vmem] * 6,
        out_specs=vmem,
        scratch_shapes=[
            pltpu.VMEM((2, BLOCKS, 384, 128), jnp.bfloat16),
            pltpu.VMEM((2, OWN + EDGE, 1024), jnp.bfloat16),
            pltpu.VMEM((4, 2, OWN + EDGE, 128), jnp.bfloat16),
        ],
        compiler_params=pltpu.CompilerParams(vmem_limit_bytes=16 * 1024 * 1024),
    )(
        place,
        numbers,
        weights,
        near,
        far,
        edge,
        mine,
        other,
        observed.reshape(2, OWN, 1024),
    )
    return ratio.reshape(2, PLANES, ROWS, 1024)


def solution(mesh):
    fine = Mesh(mesh.devices.reshape(SIZES), AXES)
    gz = ("z", "x", "core")
    in_specs = (P(gz, "gy", "view"), P("view", gz, "gy", None), P("view", gz), P(), P(), P())
    out_specs = P("view", gz, "gy", None)
    return jax.shard_map(shards, mesh=fine, in_specs=in_specs, out_specs=out_specs, check_vma=False)
```

```python
import itertools

import jax
import jax.numpy as jnp
from jax import lax
from jax.experimental import pallas as pl
from jax.experimental.pallas import tpu as pltpu
from jax.sharding import Mesh, PartitionSpec as P

PLANES, ROWS, HALO = 4, 32, 4
OWN = PLANES * ROWS
EDGE = PLANES * HALO
BLOCKS = 8
BAND = 3
AHEAD = 5
AXES = ("z", "x", "core", "view", "gy")
SIZES = (12, 4, 2, 4, 2)


def fused(place, numbers, weights, own, one, two, three, edge, mine, other, observed, ratio, dense, flat, seen):
    view, side, core = place[0], place[1], place[2]
    for k, part in enumerate((own, one, two, three)):
        seen[view ^ k, :, :OWN] = part[:, :OWN]
        seen[view ^ k ^ 3, :, OWN:] = jnp.where(place[3] == 1, part[:, OWN:], edge[k])
    dense[...] = jnp.zeros_like(dense)
    for w in range(2):
        for i in range(2 * BLOCKS):
            j, half = i // 2, i % 2
            for k in range(BAND):
                shift = (numbers[w, BLOCKS + i * BAND + k] - (2 * j - 2)) & 15
                base = shift * 64
                lanes = pl.ds(64 * half, 64)
                q = i * BAND + k
                s = q % 4 * 12 + q // 4
                dense[w, j, pl.ds(pl.multiple_of(base + 32 * core, 32), 32), lanes] = mine[
                    s, :, 64 * w : 64 * w + 64
                ]
                dense[w, j, pl.ds(pl.multiple_of(base + 32 * (1 - core), 32), 32), lanes] = other[
                    s, :, 64 * w : 64 * w + 64
                ]

    def block(w, j):
        b = numbers[w, j % BLOCKS]
        return seen[b // 2, b % 2]

    for w in range(2):
        for j in range(BLOCKS):
            wide = jnp.concatenate([block(w, j + BLOCKS - 1), block(w, j), block(w, j + 1)], axis=1)
            flat[w, :, 128 * j : 128 * j + 128] = jnp.dot(
                wide, dense[w, j], preferred_element_type=jnp.float32
            ).astype(jnp.bfloat16)

    shape = (OWN, OWN + EDGE)
    row = lax.broadcasted_iota(jnp.int32, shape, 0)
    col = lax.broadcasted_iota(jnp.int32, shape, 1)
    outer = col - OWN
    spot = jnp.where(col < OWN, col & (ROWS - 1), (outer & (HALO - 1)) + jnp.where(side == 0, ROWS, -HALO))
    plane = jnp.where(col < OWN, col >> 5, outer >> 2)
    tap = jnp.where(plane == (row >> 5), spot - (row & (ROWS - 1)) + HALO, -1)
    for w in range(2):
        mix = jnp.zeros(shape, jnp.float32)
        for t in range(2 * HALO + 1):
            mix = jnp.where(tap == t, weights[w, t], mix)
        high = mix.astype(jnp.bfloat16)
        low = (mix - high.astype(jnp.float32)).astype(jnp.bfloat16)
        lateral = flat[w]
        blurred = jnp.dot(high, lateral, preferred_element_type=jnp.float32)
        blurred = blurred + jnp.dot(low, lateral, preferred_element_type=jnp.float32)
        ratio[w] = observed[w] / blurred


def early(z):
    return z < AHEAD


def permute(array, route, chosen=lambda z: True):
    pairs = []
    for z, x, core, v, gy in itertools.product(*map(range, SIZES)):
        if chosen(z):
            to, across = route(v, gy)
            base = ((z * SIZES[1] + x) * SIZES[2] + core) * SIZES[3]
            pairs.append(((base + v) * SIZES[4] + gy, (base + to) * SIZES[4] + across))
    return lax.ppermute(array, AXES, pairs)


def mirror(v, gy):
    return 3 - v, 1 - gy


def shards(estimate, observed, psf_blocks, kernel_y, block_source, psf_columns):
    side = lax.axis_index("gy")
    place = [lax.axis_index("view"), side, lax.axis_index("core"), early(lax.axis_index("z"))]
    place = jnp.stack([jnp.asarray(entry, jnp.int32) for entry in place])
    shard = psf_blocks.reshape(2, 32, 64).transpose(1, 0, 2).reshape(1, 32, 128)
    spread = jnp.broadcast_to(shard, (12, 32, 128))
    begin = jnp.where(side == 0, ROWS - HALO, 0)
    ahead = permute(lax.dynamic_slice_in_dim(estimate, begin, HALO, 1), mirror, early)
    ahead, spread, estimate = lax.optimization_barrier((ahead, spread, estimate))
    along = lax.all_to_all(spread, "z", 0, 0, tiled=True)
    slab = jnp.concatenate([estimate.reshape(OWN, 2, 128), ahead.reshape(EDGE, 2, 128)], axis=0)
    slab = slab.transpose(1, 0, 2)
    two = permute(slab, lambda v, gy: (v ^ 2, gy))
    three = permute(slab, lambda v, gy: (v ^ 3, gy))
    one = permute(slab, lambda v, gy: (v ^ 1, gy))
    along, two, three = lax.optimization_barrier((along, two, three))
    spread, one = lax.optimization_barrier((jnp.broadcast_to(along[None], (4, 12, 32, 128)), one))
    mine = lax.all_to_all(spread, "x", 0, 0, tiled=True)
    mine, slab, one, two, three = lax.optimization_barrier((mine, slab, one, two, three))
    rows = [part.reshape(2, 18, 8, 128) for part in (slab, one, two, three)]
    upper = jnp.stack([part[:, 0:16:4, :HALO] for part in rows])
    lower = jnp.stack([part[:, 3:16:4, HALO:] for part in rows])
    rows = jnp.where(side == 0, lower, upper)
    edge = permute(rows, mirror, lambda z: not early(z)).reshape(4, 2, EDGE, 128)
    mine = mine.reshape(48, 32, 128)
    kernel_y, block_source, psf_columns = lax.optimization_barrier(
        (kernel_y, block_source, psf_columns, mine)
    )[:3]
    first = 2 * lax.axis_index("view")
    numbers = jnp.concatenate([block_source, psf_columns.reshape(8, 48)], axis=1)
    numbers = lax.dynamic_slice_in_dim(numbers, first, 2, 0)
    weights = lax.dynamic_slice_in_dim(kernel_y, first, 2, 0)
    other = lax.ppermute(mine, "core", [(0, 1), (1, 0)])
    smem = pl.BlockSpec(memory_space=pltpu.SMEM)
    vmem = pl.BlockSpec(memory_space=pltpu.VMEM)
    ratio = pl.pallas_call(
        fused,
        out_shape=jax.ShapeDtypeStruct((2, OWN, 1024), jnp.float32),
        in_specs=[smem] * 3 + [vmem] * 8,
        out_specs=vmem,
        scratch_shapes=[
            pltpu.VMEM((2, BLOCKS, 384, 128), jnp.bfloat16),
            pltpu.VMEM((2, OWN + EDGE, 1024), jnp.bfloat16),
            pltpu.VMEM((4, 2, OWN + EDGE, 128), jnp.bfloat16),
        ],
        compiler_params=pltpu.CompilerParams(vmem_limit_bytes=16 * 1024 * 1024),
    )(
        place,
        numbers,
        weights,
        slab,
        one,
        two,
        three,
        edge,
        mine,
        other,
        observed.reshape(2, OWN, 1024),
    )
    return ratio.reshape(2, PLANES, ROWS, 1024)


def solution(mesh):
    fine = Mesh(mesh.devices.reshape(SIZES), AXES)
    gz = ("z", "x", "core")
    in_specs = (P(gz, "gy", "view"), P("view", gz, "gy", None), P("view", gz), P(), P(), P())
    out_specs = P("view", gz, "gy", None)
    return jax.shard_map(shards, mesh=fine, in_specs=in_specs, out_specs=out_specs, check_vma=False)
```

```python
import itertools

import jax
import jax.numpy as jnp
from jax import lax
from jax.experimental import pallas as pl
from jax.experimental.pallas import tpu as pltpu
from jax.sharding import Mesh, PartitionSpec as P

PLANES, ROWS, HALO = 4, 32, 4
OWN = PLANES * ROWS
EDGE = PLANES * HALO
BLOCKS = 8
BAND = 3
AHEAD = 7
AXES = ("z", "x", "core", "view", "gy")
SIZES = (12, 4, 2, 4, 2)


def fused(place, numbers, weights, own, one, two, three, edge, mine, other, observed, ratio, dense, flat, seen):
    view, side, core = place[0], place[1], place[2]
    for k, part in enumerate((own, one, two, three)):
        seen[view ^ k, :, :OWN] = part[:, :OWN]
        seen[view ^ k ^ 3, :, OWN:] = jnp.where(place[3] == 1, part[:, OWN:], edge[k])
    dense[...] = jnp.zeros_like(dense)
    for w in range(2):
        for i in range(2 * BLOCKS):
            j, half = i // 2, i % 2
            for k in range(BAND):
                shift = (numbers[w, BLOCKS + i * BAND + k] - (2 * j - 2)) & 15
                base = shift * 64
                lanes = pl.ds(64 * half, 64)
                q = i * BAND + k
                s = q % 4 * 12 + q // 4
                dense[w, j, pl.ds(pl.multiple_of(base + 32 * core, 32), 32), lanes] = mine[
                    s, :, 64 * w : 64 * w + 64
                ]
                dense[w, j, pl.ds(pl.multiple_of(base + 32 * (1 - core), 32), 32), lanes] = other[
                    s, :, 64 * w : 64 * w + 64
                ]

    def block(w, j):
        b = numbers[w, j % BLOCKS]
        return seen[b // 2, b % 2]

    for w in range(2):
        for j in range(BLOCKS):
            wide = jnp.concatenate([block(w, j + BLOCKS - 1), block(w, j), block(w, j + 1)], axis=1)
            flat[w, :, 128 * j : 128 * j + 128] = jnp.dot(
                wide, dense[w, j], preferred_element_type=jnp.float32
            ).astype(jnp.bfloat16)

    shape = (OWN, OWN + EDGE)
    row = lax.broadcasted_iota(jnp.int32, shape, 0)
    col = lax.broadcasted_iota(jnp.int32, shape, 1)
    outer = col - OWN
    spot = jnp.where(col < OWN, col & (ROWS - 1), (outer & (HALO - 1)) + jnp.where(side == 0, ROWS, -HALO))
    plane = jnp.where(col < OWN, col >> 5, outer >> 2)
    tap = jnp.where(plane == (row >> 5), spot - (row & (ROWS - 1)) + HALO, -1)
    for w in range(2):
        mix = jnp.zeros(shape, jnp.float32)
        for t in range(2 * HALO + 1):
            mix = jnp.where(tap == t, weights[w, t], mix)
        high = mix.astype(jnp.bfloat16)
        low = (mix - high.astype(jnp.float32)).astype(jnp.bfloat16)
        lateral = flat[w]
        blurred = jnp.dot(high, lateral, preferred_element_type=jnp.float32)
        blurred = blurred + jnp.dot(low, lateral, preferred_element_type=jnp.float32)
        ratio[w] = observed[w] / blurred


def early(z):
    return z < AHEAD


def permute(array, route, chosen=lambda z: True):
    pairs = []
    for z, x, core, v, gy in itertools.product(*map(range, SIZES)):
        if chosen(z):
            to, across = route(v, gy)
            base = ((z * SIZES[1] + x) * SIZES[2] + core) * SIZES[3]
            pairs.append(((base + v) * SIZES[4] + gy, (base + to) * SIZES[4] + across))
    return lax.ppermute(array, AXES, pairs)


def mirror(v, gy):
    return 3 - v, 1 - gy


def shards(estimate, observed, psf_blocks, kernel_y, block_source, psf_columns):
    side = lax.axis_index("gy")
    place = [lax.axis_index("view"), side, lax.axis_index("core"), early(lax.axis_index("z"))]
    place = jnp.stack([jnp.asarray(entry, jnp.int32) for entry in place])
    shard = psf_blocks.reshape(2, 32, 64).transpose(1, 0, 2).reshape(1, 32, 128)
    spread = jnp.broadcast_to(shard, (12, 32, 128))
    begin = jnp.where(side == 0, ROWS - HALO, 0)
    ahead = lax.dynamic_slice_in_dim(estimate, begin, HALO, 1)
    ahead, spread, estimate = lax.optimization_barrier((ahead, spread, estimate))
    ahead = permute(ahead, mirror, early)
    ahead, block_source, psf_columns = lax.optimization_barrier((ahead, block_source, psf_columns))
    first = 2 * lax.axis_index("view")
    numbers = jnp.concatenate([block_source, psf_columns.reshape(8, 48)], axis=1)
    numbers = lax.dynamic_slice_in_dim(numbers, first, 2, 0)
    along = lax.all_to_all(spread, "z", 0, 0, tiled=True)
    slab = jnp.concatenate([estimate.reshape(OWN, 2, 128), ahead.reshape(EDGE, 2, 128)], axis=0)
    slab = slab.transpose(1, 0, 2)
    two = permute(slab, lambda v, gy: (v ^ 2, gy))
    three = permute(slab, lambda v, gy: (v ^ 3, gy))
    along, two, three, slab, numbers = lax.optimization_barrier((along, two, three, slab, numbers))
    mine = lax.all_to_all(jnp.broadcast_to(along[None], (4, 12, 32, 128)), "x", 0, 0, tiled=True)
    one = permute(slab, lambda v, gy: (v ^ 1, gy))
    mine, slab, one, two, three = lax.optimization_barrier((mine, slab, one, two, three))
    rows = [part.reshape(2, 18, 8, 128) for part in (slab, one, two, three)]
    upper = jnp.stack([part[:, 0:16:4, :HALO] for part in rows])
    lower = jnp.stack([part[:, 3:16:4, HALO:] for part in rows])
    rows = jnp.where(side == 0, lower, upper)
    edge = permute(rows, mirror, lambda z: not early(z)).reshape(4, 2, EDGE, 128)
    mine = mine.reshape(48, 32, 128)
    kernel_y, _ = lax.optimization_barrier((kernel_y, mine))
    weights = lax.dynamic_slice_in_dim(kernel_y, first, 2, 0)
    other = lax.ppermute(mine, "core", [(0, 1), (1, 0)])
    smem = pl.BlockSpec(memory_space=pltpu.SMEM)
    vmem = pl.BlockSpec(memory_space=pltpu.VMEM)
    ratio = pl.pallas_call(
        fused,
        out_shape=jax.ShapeDtypeStruct((2, OWN, 1024), jnp.float32),
        in_specs=[smem] * 3 + [vmem] * 8,
        out_specs=vmem,
        scratch_shapes=[
            pltpu.VMEM((2, BLOCKS, 384, 128), jnp.bfloat16),
            pltpu.VMEM((2, OWN + EDGE, 1024), jnp.bfloat16),
            pltpu.VMEM((4, 2, OWN + EDGE, 128), jnp.bfloat16),
        ],
        compiler_params=pltpu.CompilerParams(vmem_limit_bytes=16 * 1024 * 1024),
    )(
        place,
        numbers,
        weights,
        slab,
        one,
        two,
        three,
        edge,
        mine,
        other,
        observed.reshape(2, OWN, 1024),
    )
    return ratio.reshape(2, PLANES, ROWS, 1024)


def solution(mesh):
    fine = Mesh(mesh.devices.reshape(SIZES), AXES)
    gz = ("z", "x", "core")
    in_specs = (P(gz, "gy", "view"), P("view", gz, "gy", None), P("view", gz), P(), P(), P())
    out_specs = P("view", gz, "gy", None)
    return jax.shard_map(shards, mesh=fine, in_specs=in_specs, out_specs=out_specs, check_vma=False)
```

```python
import itertools

import jax
import jax.numpy as jnp
from jax import lax
from jax.experimental import pallas as pl
from jax.experimental.pallas import tpu as pltpu
from jax.sharding import Mesh, PartitionSpec as P

PLANES, ROWS, HALO = 4, 32, 4
OWN = PLANES * ROWS
EDGE = PLANES * HALO
BLOCKS = 8
BAND = 3
AHEAD = 5
AXES = ("z", "x", "core", "view", "gy")
SIZES = (12, 4, 2, 4, 2)


def fused(place, numbers, weights, own, one, two, three, edge, mine, other, observed, ratio, dense, seen, done, sems):
    view, side, core = place[0], place[1], place[2]
    for k, part in enumerate((own, one, two, three)):
        seen[view ^ k, :, :OWN] = part[:, :OWN]
        seen[view ^ k ^ 3, :, OWN:] = jnp.where(place[3] == 1, part[:, OWN:], edge[k])

    def build(w):
        dense[w] = jnp.zeros_like(dense[w])
        for i in range(2 * BLOCKS):
            j, quarter = i // 4, i % 4
            for k in range(BAND):
                shift = (numbers[w, BLOCKS + i * BAND + k] - (4 * j - 2)) & 15
                base = shift * 64
                lanes = pl.ds(64 * quarter, 64)
                q = i * BAND + k
                s = q % 4 * 12 + q // 4
                dense[w, j, pl.ds(pl.multiple_of(base + 32 * core, 32), 32), lanes] = mine[
                    s, :, 64 * w : 64 * w + 64
                ]
                dense[w, j, pl.ds(pl.multiple_of(base + 32 * (1 - core), 32), 32), lanes] = other[
                    s, :, 64 * w : 64 * w + 64
                ]

    build(0)

    def block(w, j):
        b = numbers[w, j % BLOCKS]
        return seen[b // 2, b % 2]

    shape = (OWN, OWN + EDGE)
    row = lax.broadcasted_iota(jnp.int32, shape, 0)
    col = lax.broadcasted_iota(jnp.int32, shape, 1)
    outer = col - OWN
    spot = jnp.where(col < OWN, col & (ROWS - 1), (outer & (HALO - 1)) + jnp.where(side == 0, ROWS, -HALO))
    plane = jnp.where(col < OWN, col >> 5, outer >> 2)
    tap = jnp.where(plane == (row >> 5), spot - (row & (ROWS - 1)) + HALO, -1)
    mixes = []
    for w in range(2):
        mix = jnp.zeros(shape, jnp.float32)
        for t in range(2 * HALO + 1):
            mix = jnp.where(tap == t, weights[w, t], mix)
        high = mix.astype(jnp.bfloat16)
        low = (mix - high.astype(jnp.float32)).astype(jnp.bfloat16)
        mixes.append((high, low))

    copies = []

    def lateral(n):
        w, j = n // 4, n % 4
        wide = jnp.concatenate([block(w, 2 * j + BLOCKS + s) for s in (-1, 0, 1, 2)], axis=1)
        return jnp.dot(wide, dense[w, j], preferred_element_type=jnp.float32).astype(jnp.bfloat16)

    def finish(n, rows):
        w, j = n // 4, n % 4
        lanes = slice(256 * j, 256 * j + 256)
        blurred = jnp.dot(mixes[w][0], rows, preferred_element_type=jnp.float32)
        blurred = blurred + jnp.dot(mixes[w][1], rows, preferred_element_type=jnp.float32)
        done[w, :, lanes] = observed[w, :, lanes] / blurred
        copies.append(pltpu.make_async_copy(done.at[w, :, lanes], ratio.at[w, :, lanes], sems.at[n]))
        copies[-1].start()

    rows = lateral(0)
    for n in range(8):
        if n == 0:
            build(1)
        after = lateral(n + 1) if n < 7 else None
        finish(n, rows)
        rows = after
    for copy in copies:
        copy.wait()


def early(z):
    return z < AHEAD


def permute(array, route, chosen=lambda z: True):
    pairs = []
    for z, x, core, v, gy in itertools.product(*map(range, SIZES)):
        if chosen(z):
            to, across = route(v, gy)
            base = ((z * SIZES[1] + x) * SIZES[2] + core) * SIZES[3]
            pairs.append(((base + v) * SIZES[4] + gy, (base + to) * SIZES[4] + across))
    return lax.ppermute(array, AXES, pairs)


def mirror(v, gy):
    return 3 - v, 1 - gy


def shards(estimate, observed, psf_blocks, kernel_y, block_source, psf_columns):
    side = lax.axis_index("gy")
    place = [lax.axis_index("view"), side, lax.axis_index("core"), early(lax.axis_index("z"))]
    place = jnp.stack([jnp.asarray(entry, jnp.int32) for entry in place])
    shard = psf_blocks.reshape(2, 32, 64).transpose(1, 0, 2).reshape(1, 32, 128)
    spread = jnp.broadcast_to(shard, (12, 32, 128))
    begin = jnp.where(side == 0, ROWS - HALO, 0)
    ahead = lax.dynamic_slice_in_dim(estimate, begin, HALO, 1)
    ahead, spread, estimate = lax.optimization_barrier((ahead, spread, estimate))
    ahead = permute(ahead, mirror, early)
    ahead, block_source, psf_columns = lax.optimization_barrier((ahead, block_source, psf_columns))
    first = 2 * lax.axis_index("view")
    numbers = jnp.concatenate([block_source, psf_columns.reshape(8, 48)], axis=1)
    numbers = lax.dynamic_slice_in_dim(numbers, first, 2, 0)
    along = lax.all_to_all(spread, "z", 0, 0, tiled=True)
    slab = jnp.concatenate([estimate.reshape(OWN, 2, 128), ahead.reshape(EDGE, 2, 128)], axis=0)
    slab = slab.transpose(1, 0, 2)
    two = permute(slab, lambda v, gy: (v ^ 2, gy))
    three = permute(slab, lambda v, gy: (v ^ 3, gy))
    along, two, three, slab, numbers = lax.optimization_barrier((along, two, three, slab, numbers))
    mine = lax.all_to_all(jnp.broadcast_to(along[None], (4, 12, 32, 128)), "x", 0, 0, tiled=True)
    one = permute(slab, lambda v, gy: (v ^ 1, gy))
    mine, slab, one, two, three = lax.optimization_barrier((mine, slab, one, two, three))
    rows = [part.reshape(2, 18, 8, 128) for part in (slab, one, two, three)]
    upper = jnp.stack([part[:, 0:16:4, :HALO] for part in rows])
    lower = jnp.stack([part[:, 3:16:4, HALO:] for part in rows])
    rows = jnp.where(side == 0, lower, upper)
    edge = permute(rows, mirror, lambda z: not early(z)).reshape(4, 2, EDGE, 128)
    mine = mine.reshape(48, 32, 128)
    kernel_y, _ = lax.optimization_barrier((kernel_y, mine))
    weights = lax.dynamic_slice_in_dim(kernel_y, first, 2, 0)
    other = lax.ppermute(mine, "core", [(0, 1), (1, 0)])
    smem = pl.BlockSpec(memory_space=pltpu.SMEM)
    vmem = pl.BlockSpec(memory_space=pltpu.VMEM)
    ratio = pl.pallas_call(
        fused,
        out_shape=jax.ShapeDtypeStruct((2, OWN, 1024), jnp.float32),
        in_specs=[smem] * 3 + [vmem] * 8,
        out_specs=pl.BlockSpec(memory_space=pl.ANY),
        scratch_shapes=[
            pltpu.VMEM((2, BLOCKS // 2, 512, 256), jnp.bfloat16),
            pltpu.VMEM((4, 2, OWN + EDGE, 128), jnp.bfloat16),
            pltpu.VMEM((2, OWN, 1024), jnp.float32),
            pltpu.SemaphoreType.DMA((8,)),
        ],
        compiler_params=pltpu.CompilerParams(vmem_limit_bytes=16 * 1024 * 1024),
    )(
        place,
        numbers,
        weights,
        slab,
        one,
        two,
        three,
        edge,
        mine,
        other,
        observed.reshape(2, OWN, 1024),
    )
    return ratio.reshape(2, PLANES, ROWS, 1024)


def solution(mesh):
    fine = Mesh(mesh.devices.reshape(SIZES), AXES)
    gz = ("z", "x", "core")
    in_specs = (P(gz, "gy", "view"), P("view", gz, "gy", None), P("view", gz), P(), P(), P())
    out_specs = P("view", gz, "gy", None)
    return jax.shard_map(shards, mesh=fine, in_specs=in_specs, out_specs=out_specs, check_vma=False)
```

```python
import itertools

import jax
import jax.numpy as jnp
from jax import lax
from jax.experimental import pallas as pl
from jax.experimental.pallas import tpu as pltpu
from jax.sharding import Mesh, PartitionSpec as P

PLANES, ROWS, HALO = 4, 32, 4
OWN = PLANES * ROWS
EDGE = PLANES * HALO
BLOCKS = 8
BAND = 3
AHEAD = 6
AXES = ("z", "x", "core", "view", "gy")
SIZES = (12, 4, 2, 4, 2)


def fused(place, numbers, weights, own, one, two, three, edge, mine, other, observed, ratio, dense, seen, done, sems):
    view, side, core = place[0], place[1], place[2]
    for k, part in enumerate((own, one, two, three)):
        seen[view ^ k, :, :OWN] = part[:, :OWN]
        seen[view ^ k ^ 3, :, OWN:] = jnp.where(place[3] == 1, part[:, OWN:], edge[k])

    def build(w):
        dense[w] = jnp.zeros_like(dense[w])
        for i in range(2 * BLOCKS):
            j, quarter = i // 4, i % 4
            for k in range(BAND):
                shift = (numbers[w, BLOCKS + i * BAND + k] - (4 * j - 2)) & 15
                base = shift * 64
                lanes = pl.ds(64 * quarter, 64)
                q = i * BAND + k
                s = q % 4 * 12 + q // 4
                dense[w, j, pl.ds(pl.multiple_of(base + 32 * core, 32), 32), lanes] = mine[
                    s, :, 64 * w : 64 * w + 64
                ]
                dense[w, j, pl.ds(pl.multiple_of(base + 32 * (1 - core), 32), 32), lanes] = other[
                    s, :, 64 * w : 64 * w + 64
                ]

    build(0)

    def block(w, j):
        b = numbers[w, j % BLOCKS]
        return seen[b // 2, b % 2]

    shape = (OWN, OWN + EDGE)
    row = lax.broadcasted_iota(jnp.int32, shape, 0)
    col = lax.broadcasted_iota(jnp.int32, shape, 1)
    outer = col - OWN
    spot = jnp.where(col < OWN, col & (ROWS - 1), (outer & (HALO - 1)) + jnp.where(side == 0, ROWS, -HALO))
    plane = jnp.where(col < OWN, col >> 5, outer >> 2)
    tap = jnp.where(plane == (row >> 5), spot - (row & (ROWS - 1)) + HALO, -1)
    mixes = []
    for w in range(2):
        mix = jnp.zeros(shape, jnp.float32)
        for t in range(2 * HALO + 1):
            mix = jnp.where(tap == t, weights[w, t], mix)
        high = mix.astype(jnp.bfloat16)
        low = (mix - high.astype(jnp.float32)).astype(jnp.bfloat16)
        mixes.append((high, low))

    copies = []

    def lateral(n):
        w, j = n // 4, n % 4
        wide = jnp.concatenate([block(w, 2 * j + BLOCKS + s) for s in (-1, 0, 1, 2)], axis=1)
        return jnp.dot(wide, dense[w, j], preferred_element_type=jnp.float32).astype(jnp.bfloat16)

    def finish(n, rows):
        w, j = n // 4, n % 4
        lanes = slice(256 * j, 256 * j + 256)
        blurred = jnp.dot(mixes[w][0], rows, preferred_element_type=jnp.float32)
        blurred = blurred + jnp.dot(mixes[w][1], rows, preferred_element_type=jnp.float32)
        done[w, :, lanes] = observed[w, :, lanes] / blurred
        copies.append(pltpu.make_async_copy(done.at[w, :, lanes], ratio.at[w, :, lanes], sems.at[n]))
        copies[-1].start()

    rows = lateral(0)
    for n in range(8):
        if n == 0:
            build(1)
        after = lateral(n + 1) if n < 7 else None
        finish(n, rows)
        rows = after
    for copy in copies:
        copy.wait()


def early(z):
    return z < AHEAD


def permute(array, route, chosen=lambda z: True):
    pairs = []
    for z, x, core, v, gy in itertools.product(*map(range, SIZES)):
        if chosen(z):
            to, across = route(v, gy)
            base = ((z * SIZES[1] + x) * SIZES[2] + core) * SIZES[3]
            pairs.append(((base + v) * SIZES[4] + gy, (base + to) * SIZES[4] + across))
    return lax.ppermute(array, AXES, pairs)


def mirror(v, gy):
    return 3 - v, 1 - gy


def shards(estimate, observed, psf_blocks, kernel_y, block_source, psf_columns):
    side = lax.axis_index("gy")
    place = [lax.axis_index("view"), side, lax.axis_index("core"), early(lax.axis_index("z"))]
    place = jnp.stack([jnp.asarray(entry, jnp.int32) for entry in place])
    shard = psf_blocks.reshape(2, 32, 64).transpose(1, 0, 2).reshape(1, 32, 128)
    spread = jnp.broadcast_to(shard, (12, 32, 128))
    begin = jnp.where(side == 0, ROWS - HALO, 0)
    ahead = lax.dynamic_slice_in_dim(estimate, begin, HALO, 1)
    ahead, spread, estimate = lax.optimization_barrier((ahead, spread, estimate))
    ahead = permute(ahead, mirror, early)
    ahead, block_source, psf_columns = lax.optimization_barrier((ahead, block_source, psf_columns))
    first = 2 * lax.axis_index("view")
    numbers = jnp.concatenate([block_source, psf_columns.reshape(8, 48)], axis=1)
    numbers = lax.dynamic_slice_in_dim(numbers, first, 2, 0)
    along = lax.all_to_all(spread, "z", 0, 0, tiled=True)
    slab = jnp.concatenate([estimate.reshape(OWN, 2, 128), ahead.reshape(EDGE, 2, 128)], axis=0)
    slab = slab.transpose(1, 0, 2)
    two = permute(slab, lambda v, gy: (v ^ 2, gy))
    one = permute(slab, lambda v, gy: (v ^ 1, gy))
    along, one, two, slab, numbers = lax.optimization_barrier((along, one, two, slab, numbers))
    mine = lax.all_to_all(jnp.broadcast_to(along[None], (4, 12, 32, 128)), "x", 0, 0, tiled=True)
    three = permute(slab, lambda v, gy: (v ^ 3, gy))
    mine, slab, one, two, three = lax.optimization_barrier((mine, slab, one, two, three))
    rows = [part.reshape(2, 18, 8, 128) for part in (slab, one, two, three)]
    upper = jnp.stack([part[:, 0:16:4, :HALO] for part in rows])
    lower = jnp.stack([part[:, 3:16:4, HALO:] for part in rows])
    rows = jnp.where(side == 0, lower, upper)
    edge = permute(rows, mirror, lambda z: not early(z)).reshape(4, 2, EDGE, 128)
    mine = mine.reshape(48, 32, 128)
    kernel_y, _ = lax.optimization_barrier((kernel_y, mine))
    weights = lax.dynamic_slice_in_dim(kernel_y, first, 2, 0)
    other = lax.ppermute(mine, "core", [(0, 1), (1, 0)])
    smem = pl.BlockSpec(memory_space=pltpu.SMEM)
    vmem = pl.BlockSpec(memory_space=pltpu.VMEM)
    ratio = pl.pallas_call(
        fused,
        out_shape=jax.ShapeDtypeStruct((2, OWN, 1024), jnp.float32),
        in_specs=[smem] * 3 + [vmem] * 8,
        out_specs=pl.BlockSpec(memory_space=pl.ANY),
        scratch_shapes=[
            pltpu.VMEM((2, BLOCKS // 2, 512, 256), jnp.bfloat16),
            pltpu.VMEM((4, 2, OWN + EDGE, 128), jnp.bfloat16),
            pltpu.VMEM((2, OWN, 1024), jnp.float32),
            pltpu.SemaphoreType.DMA((8,)),
        ],
        compiler_params=pltpu.CompilerParams(vmem_limit_bytes=16 * 1024 * 1024),
    )(
        place,
        numbers,
        weights,
        slab,
        one,
        two,
        three,
        edge,
        mine,
        other,
        observed.reshape(2, OWN, 1024),
    )
    return ratio.reshape(2, PLANES, ROWS, 1024)


def solution(mesh):
    fine = Mesh(mesh.devices.reshape(SIZES), AXES)
    gz = ("z", "x", "core")
    in_specs = (P(gz, "gy", "view"), P("view", gz, "gy", None), P("view", gz), P(), P(), P())
    out_specs = P("view", gz, "gy", None)
    return jax.shard_map(shards, mesh=fine, in_specs=in_specs, out_specs=out_specs, check_vma=False)
```

```python
import itertools

import jax
import jax.numpy as jnp
from jax import lax
from jax.experimental import pallas as pl
from jax.experimental.pallas import tpu as pltpu
from jax.sharding import Mesh, PartitionSpec as P

PLANES, ROWS, HALO = 4, 32, 4
OWN = PLANES * ROWS
EDGE = PLANES * HALO
BLOCKS = 8
BAND = 3
AHEAD = 22
AXES = ("z", "x", "core", "view", "gy")
SIZES = (12, 4, 2, 4, 2)


def fused(place, numbers, weights, own, one, two, three, edge, mine, other, observed, ratio, dense, seen, done, sems):
    view, side, core = place[0], place[1], place[2]
    for k, part in enumerate((own, one, two, three)):
        seen[view ^ k, :, :OWN] = part[:, :OWN]
        seen[view ^ k ^ 3, :, OWN:] = jnp.where(place[3] == 1, part[:, OWN:], edge[k])

    def build(w):
        dense[w] = jnp.zeros_like(dense[w])
        for i in range(2 * BLOCKS):
            j, quarter = i // 4, i % 4
            for k in range(BAND):
                shift = (numbers[w, BLOCKS + i * BAND + k] - (4 * j - 2)) & 15
                base = shift * 64
                lanes = pl.ds(64 * quarter, 64)
                q = i * BAND + k
                s = q % 4 * 12 + q // 4
                dense[w, j, pl.ds(pl.multiple_of(base + 32 * core, 32), 32), lanes] = mine[
                    s, :, 64 * w : 64 * w + 64
                ]
                dense[w, j, pl.ds(pl.multiple_of(base + 32 * (1 - core), 32), 32), lanes] = other[
                    s, :, 64 * w : 64 * w + 64
                ]

    build(0)

    def block(w, j):
        b = numbers[w, j % BLOCKS]
        return seen[b // 2, b % 2]

    shape = (OWN, OWN + EDGE)
    row = lax.broadcasted_iota(jnp.int32, shape, 0)
    col = lax.broadcasted_iota(jnp.int32, shape, 1)
    outer = col - OWN
    spot = jnp.where(col < OWN, col & (ROWS - 1), (outer & (HALO - 1)) + jnp.where(side == 0, ROWS, -HALO))
    plane = jnp.where(col < OWN, col >> 5, outer >> 2)
    tap = jnp.where(plane == (row >> 5), spot - (row & (ROWS - 1)) + HALO, -1)
    mixes = []
    for w in range(2):
        mix = jnp.zeros(shape, jnp.float32)
        for t in range(2 * HALO + 1):
            mix = jnp.where(tap == t, weights[w, t], mix)
        high = mix.astype(jnp.bfloat16)
        low = (mix - high.astype(jnp.float32)).astype(jnp.bfloat16)
        mixes.append((high, low))

    copies = []

    def lateral(n):
        w, j = n // 4, n % 4
        wide = jnp.concatenate([block(w, 2 * j + BLOCKS + s) for s in (-1, 0, 1, 2)], axis=1)
        return jnp.dot(wide, dense[w, j], preferred_element_type=jnp.float32).astype(jnp.bfloat16)

    def finish(n, rows):
        w, j = n // 4, n % 4
        lanes = slice(256 * j, 256 * j + 256)
        blurred = jnp.dot(mixes[w][0], rows, preferred_element_type=jnp.float32)
        blurred = blurred + jnp.dot(mixes[w][1], rows, preferred_element_type=jnp.float32)
        done[w, :, lanes] = observed[w, :, lanes] / blurred
        copies.append(pltpu.make_async_copy(done.at[w, :, lanes], ratio.at[w, :, lanes], sems.at[n]))
        copies[-1].start()

    rows = lateral(0)
    for n in range(8):
        if n == 0:
            build(1)
        after = lateral(n + 1) if n < 7 else None
        finish(n, rows)
        rows = after
    for copy in copies:
        copy.wait()


def early(z, x):
    return z * SIZES[1] + x < AHEAD


def permute(array, route, chosen=lambda *at: True):
    pairs = []
    for z, x, core, v, gy in itertools.product(*map(range, SIZES)):
        if chosen(z, x):
            to, across = route(v, gy)
            base = ((z * SIZES[1] + x) * SIZES[2] + core) * SIZES[3]
            pairs.append(((base + v) * SIZES[4] + gy, (base + to) * SIZES[4] + across))
    return lax.ppermute(array, AXES, pairs)


def mirror(v, gy):
    return 3 - v, 1 - gy


def shards(estimate, observed, psf_blocks, kernel_y, block_source, psf_columns):
    side = lax.axis_index("gy")
    place = [lax.axis_index("view"), side, lax.axis_index("core"), early(lax.axis_index("z"), lax.axis_index("x"))]
    place = jnp.stack([jnp.asarray(entry, jnp.int32) for entry in place])
    shard = psf_blocks.reshape(2, 32, 64).transpose(1, 0, 2).reshape(1, 32, 128)
    spread = jnp.broadcast_to(shard, (12, 32, 128))
    begin = jnp.where(side == 0, ROWS - HALO, 0)
    ahead = lax.dynamic_slice_in_dim(estimate, begin, HALO, 1)
    ahead, spread, estimate = lax.optimization_barrier((ahead, spread, estimate))
    ahead = permute(ahead, mirror, early)
    ahead, block_source, psf_columns = lax.optimization_barrier((ahead, block_source, psf_columns))
    first = 2 * lax.axis_index("view")
    numbers = jnp.concatenate([block_source, psf_columns.reshape(8, 48)], axis=1)
    numbers = lax.dynamic_slice_in_dim(numbers, first, 2, 0)
    along = lax.all_to_all(spread, "z", 0, 0, tiled=True)
    slab = jnp.concatenate([estimate.reshape(OWN, 2, 128), ahead.reshape(EDGE, 2, 128)], axis=0)
    slab = slab.transpose(1, 0, 2)
    two = permute(slab, lambda v, gy: (v ^ 2, gy))
    three = permute(slab, lambda v, gy: (v ^ 3, gy))
    along, two, three, slab, numbers = lax.optimization_barrier((along, two, three, slab, numbers))
    mine = lax.all_to_all(jnp.broadcast_to(along[None], (4, 12, 32, 128)), "x", 0, 0, tiled=True)
    one = permute(slab, lambda v, gy: (v ^ 1, gy))
    mine, slab, one, two, three = lax.optimization_barrier((mine, slab, one, two, three))
    rows = [part.reshape(2, 18, 8, 128) for part in (slab, one, two, three)]
    upper = jnp.stack([part[:, 0:16:4, :HALO] for part in rows])
    lower = jnp.stack([part[:, 3:16:4, HALO:] for part in rows])
    rows = jnp.where(side == 0, lower, upper)
    edge = permute(rows, mirror, lambda *at: not early(*at)).reshape(4, 2, EDGE, 128)
    mine = mine.reshape(48, 32, 128)
    kernel_y, _ = lax.optimization_barrier((kernel_y, mine))
    weights = lax.dynamic_slice_in_dim(kernel_y, first, 2, 0)
    other = lax.ppermute(mine, "core", [(0, 1), (1, 0)])
    smem = pl.BlockSpec(memory_space=pltpu.SMEM)
    vmem = pl.BlockSpec(memory_space=pltpu.VMEM)
    ratio = pl.pallas_call(
        fused,
        out_shape=jax.ShapeDtypeStruct((2, OWN, 1024), jnp.float32),
        in_specs=[smem] * 3 + [vmem] * 8,
        out_specs=pl.BlockSpec(memory_space=pl.ANY),
        scratch_shapes=[
            pltpu.VMEM((2, BLOCKS // 2, 512, 256), jnp.bfloat16),
            pltpu.VMEM((4, 2, OWN + EDGE, 128), jnp.bfloat16),
            pltpu.VMEM((2, OWN, 1024), jnp.float32),
            pltpu.SemaphoreType.DMA((8,)),
        ],
        compiler_params=pltpu.CompilerParams(vmem_limit_bytes=16 * 1024 * 1024),
    )(
        place,
        numbers,
        weights,
        slab,
        one,
        two,
        three,
        edge,
        mine,
        other,
        observed.reshape(2, OWN, 1024),
    )
    return ratio.reshape(2, PLANES, ROWS, 1024)


def solution(mesh):
    fine = Mesh(mesh.devices.reshape(SIZES), AXES)
    gz = ("z", "x", "core")
    in_specs = (P(gz, "gy", "view"), P("view", gz, "gy", None), P("view", gz), P(), P(), P())
    out_specs = P("view", gz, "gy", None)
    return jax.shard_map(shards, mesh=fine, in_specs=in_specs, out_specs=out_specs, check_vma=False)
```

```python
import itertools

import jax
import jax.numpy as jnp
from jax import lax
from jax.experimental import pallas as pl
from jax.experimental.pallas import tpu as pltpu
from jax.sharding import Mesh, PartitionSpec as P

PLANES, ROWS, HALO = 4, 32, 4
OWN = PLANES * ROWS
EDGE = PLANES * HALO
BLOCKS = 8
BAND = 3
AHEAD = 5
AXES = ("z", "x", "core", "view", "gy")
SIZES = (12, 4, 2, 4, 2)


def fused(place, numbers, weights, own, one, two, three, edge, mine, other, observed, ratio, dense, seen, done, sems):
    view, side, core = place[0], place[1], place[2]
    for k, part in enumerate((own, one, two, three)):
        seen[view ^ k, :, :OWN] = part[:, :OWN]
        seen[view ^ k ^ 2, :, OWN:] = jnp.where(place[3] == 1, part[:, OWN:], edge[k])

    def build(w):
        dense[w] = jnp.zeros_like(dense[w])
        for i in range(2 * BLOCKS):
            j, quarter = i // 4, i % 4
            for k in range(BAND):
                shift = (numbers[w, BLOCKS + i * BAND + k] - (4 * j - 2)) & 15
                base = shift * 64
                lanes = pl.ds(64 * quarter, 64)
                q = i * BAND + k
                s = q % 4 * 12 + q // 4
                dense[w, j, pl.ds(pl.multiple_of(base + 32 * core, 32), 32), lanes] = mine[
                    s, :, 64 * w : 64 * w + 64
                ]
                dense[w, j, pl.ds(pl.multiple_of(base + 32 * (1 - core), 32), 32), lanes] = other[
                    s, :, 64 * w : 64 * w + 64
                ]

    build(0)

    def block(w, j):
        b = numbers[w, j % BLOCKS]
        return seen[b // 2, b % 2]

    shape = (OWN, OWN + EDGE)
    row = lax.broadcasted_iota(jnp.int32, shape, 0)
    col = lax.broadcasted_iota(jnp.int32, shape, 1)
    outer = col - OWN
    spot = jnp.where(col < OWN, col & (ROWS - 1), (outer & (HALO - 1)) + jnp.where(side == 0, ROWS, -HALO))
    plane = jnp.where(col < OWN, col >> 5, outer >> 2)
    tap = jnp.where(plane == (row >> 5), spot - (row & (ROWS - 1)) + HALO, -1)
    mixes = []
    for w in range(2):
        mix = jnp.zeros(shape, jnp.float32)
        for t in range(2 * HALO + 1):
            mix = jnp.where(tap == t, weights[w, t], mix)
        high = mix.astype(jnp.bfloat16)
        low = (mix - high.astype(jnp.float32)).astype(jnp.bfloat16)
        mixes.append((high, low))

    copies = []

    def lateral(n):
        w, j = n // 4, n % 4
        wide = jnp.concatenate([block(w, 2 * j + BLOCKS + s) for s in (-1, 0, 1, 2)], axis=1)
        return jnp.dot(wide, dense[w, j], preferred_element_type=jnp.float32).astype(jnp.bfloat16)

    def finish(n, rows):
        w, j = n // 4, n % 4
        lanes = slice(256 * j, 256 * j + 256)
        blurred = jnp.dot(mixes[w][0], rows, preferred_element_type=jnp.float32)
        blurred = blurred + jnp.dot(mixes[w][1], rows, preferred_element_type=jnp.float32)
        done[w, :, lanes] = observed[w, :, lanes] / blurred
        copies.append(pltpu.make_async_copy(done.at[w, :, lanes], ratio.at[w, :, lanes], sems.at[n]))
        copies[-1].start()

    rows = lateral(0)
    for n in range(8):
        if n == 0:
            build(1)
        after = lateral(n + 1) if n < 7 else None
        finish(n, rows)
        rows = after
    for copy in copies:
        copy.wait()


def early(z):
    return z < AHEAD


def permute(array, route, chosen=lambda z: True):
    pairs = []
    for z, x, core, v, gy in itertools.product(*map(range, SIZES)):
        if chosen(z):
            to, across = route(v, gy)
            base = ((z * SIZES[1] + x) * SIZES[2] + core) * SIZES[3]
            pairs.append(((base + v) * SIZES[4] + gy, (base + to) * SIZES[4] + across))
    return lax.ppermute(array, AXES, pairs)


def beyond(v, gy):
    return v ^ 2, 1 - gy


def shards(estimate, observed, psf_blocks, kernel_y, block_source, psf_columns):
    side = lax.axis_index("gy")
    place = [lax.axis_index("view"), side, lax.axis_index("core"), early(lax.axis_index("z"))]
    place = jnp.stack([jnp.asarray(entry, jnp.int32) for entry in place])
    shard = psf_blocks.reshape(2, 32, 64).transpose(1, 0, 2).reshape(1, 32, 128)
    spread = jnp.broadcast_to(shard, (12, 32, 128))
    begin = jnp.where(side == 0, ROWS - HALO, 0)
    ahead = lax.dynamic_slice_in_dim(estimate, begin, HALO, 1)
    ahead, spread, estimate = lax.optimization_barrier((ahead, spread, estimate))
    ahead = permute(ahead, beyond, early)
    ahead, block_source, psf_columns = lax.optimization_barrier((ahead, block_source, psf_columns))
    first = 2 * lax.axis_index("view")
    numbers = jnp.concatenate([block_source, psf_columns.reshape(8, 48)], axis=1)
    numbers = lax.dynamic_slice_in_dim(numbers, first, 2, 0)
    along = lax.all_to_all(spread, "z", 0, 0, tiled=True)
    slab = jnp.concatenate([estimate.reshape(OWN, 2, 128), ahead.reshape(EDGE, 2, 128)], axis=0)
    slab = slab.transpose(1, 0, 2)
    two = permute(slab, lambda v, gy: (v ^ 2, gy))
    three = permute(slab, lambda v, gy: (v ^ 3, gy))
    along, two, three, slab, numbers = lax.optimization_barrier((along, two, three, slab, numbers))
    mine = lax.all_to_all(jnp.broadcast_to(along[None], (4, 12, 32, 128)), "x", 0, 0, tiled=True)
    one = permute(slab, lambda v, gy: (v ^ 1, gy))
    mine, slab, one, two, three = lax.optimization_barrier((mine, slab, one, two, three))
    rows = [part.reshape(2, 18, 8, 128) for part in (slab, one, two, three)]
    upper = jnp.stack([part[:, 0:16:4, :HALO] for part in rows])
    lower = jnp.stack([part[:, 3:16:4, HALO:] for part in rows])
    rows = jnp.where(side == 0, lower, upper)
    edge = permute(rows, beyond, lambda z: not early(z)).reshape(4, 2, EDGE, 128)
    mine = mine.reshape(48, 32, 128)
    kernel_y, _ = lax.optimization_barrier((kernel_y, mine))
    weights = lax.dynamic_slice_in_dim(kernel_y, first, 2, 0)
    other = lax.ppermute(mine, "core", [(0, 1), (1, 0)])
    smem = pl.BlockSpec(memory_space=pltpu.SMEM)
    vmem = pl.BlockSpec(memory_space=pltpu.VMEM)
    ratio = pl.pallas_call(
        fused,
        out_shape=jax.ShapeDtypeStruct((2, OWN, 1024), jnp.float32),
        in_specs=[smem] * 3 + [vmem] * 8,
        out_specs=pl.BlockSpec(memory_space=pl.ANY),
        scratch_shapes=[
            pltpu.VMEM((2, BLOCKS // 2, 512, 256), jnp.bfloat16),
            pltpu.VMEM((4, 2, OWN + EDGE, 128), jnp.bfloat16),
            pltpu.VMEM((2, OWN, 1024), jnp.float32),
            pltpu.SemaphoreType.DMA((8,)),
        ],
        compiler_params=pltpu.CompilerParams(vmem_limit_bytes=16 * 1024 * 1024),
    )(
        place,
        numbers,
        weights,
        slab,
        one,
        two,
        three,
        edge,
        mine,
        other,
        observed.reshape(2, OWN, 1024),
    )
    return ratio.reshape(2, PLANES, ROWS, 1024)


def solution(mesh):
    fine = Mesh(mesh.devices.reshape(SIZES), AXES)
    gz = ("z", "x", "core")
    in_specs = (P(gz, "gy", "view"), P("view", gz, "gy", None), P("view", gz), P(), P(), P())
    out_specs = P("view", gz, "gy", None)
    return jax.shard_map(shards, mesh=fine, in_specs=in_specs, out_specs=out_specs, check_vma=False)
```

```python
import itertools

import jax
import jax.numpy as jnp
from jax import lax
from jax.experimental import pallas as pl
from jax.experimental.pallas import tpu as pltpu
from jax.sharding import Mesh, PartitionSpec as P

PLANES, ROWS, HALO = 4, 32, 4
OWN = PLANES * ROWS
EDGE = PLANES * HALO
BLOCKS = 8
BAND = 3
AHEAD = 5
AXES = ("z", "x", "core", "view", "gy")
SIZES = (12, 4, 2, 4, 2)


def fused(place, numbers, weights, own, one, late, two, three, edge, mine, other, observed, ratio, dense, seen, done, sems):
    view, side, core = place[0], place[1], place[2]
    soon = place[3] == 1
    for k, part in enumerate((own[...], jnp.where(soon, one[...], late[...]), two[...], three[...])):
        seen[view ^ k, :, :OWN] = part[:, :OWN]
        seen[view ^ k ^ 3, :, OWN:] = jnp.where(soon, part[:, OWN:], edge[k])

    def build(w):
        dense[w] = jnp.zeros_like(dense[w])
        for i in range(2 * BLOCKS):
            j, quarter = i // 4, i % 4
            for k in range(BAND):
                shift = (numbers[w, BLOCKS + i * BAND + k] - (4 * j - 2)) & 15
                base = shift * 64
                lanes = pl.ds(64 * quarter, 64)
                q = i * BAND + k
                s = q % 4 * 12 + q // 4
                dense[w, j, pl.ds(pl.multiple_of(base + 32 * core, 32), 32), lanes] = mine[
                    s, :, 64 * w : 64 * w + 64
                ]
                dense[w, j, pl.ds(pl.multiple_of(base + 32 * (1 - core), 32), 32), lanes] = other[
                    s, :, 64 * w : 64 * w + 64
                ]

    build(0)

    def block(w, j):
        b = numbers[w, j % BLOCKS]
        return seen[b // 2, b % 2]

    shape = (OWN, OWN + EDGE)
    row = lax.broadcasted_iota(jnp.int32, shape, 0)
    col = lax.broadcasted_iota(jnp.int32, shape, 1)
    outer = col - OWN
    spot = jnp.where(col < OWN, col & (ROWS - 1), (outer & (HALO - 1)) + jnp.where(side == 0, ROWS, -HALO))
    plane = jnp.where(col < OWN, col >> 5, outer >> 2)
    tap = jnp.where(plane == (row >> 5), spot - (row & (ROWS - 1)) + HALO, -1)
    mixes = []
    for w in range(2):
        mix = jnp.zeros(shape, jnp.float32)
        for t in range(2 * HALO + 1):
            mix = jnp.where(tap == t, weights[w, t], mix)
        high = mix.astype(jnp.bfloat16)
        low = (mix - high.astype(jnp.float32)).astype(jnp.bfloat16)
        mixes.append((high, low))

    copies = []

    def lateral(n):
        w, j = n // 4, n % 4
        wide = jnp.concatenate([block(w, 2 * j + BLOCKS + s) for s in (-1, 0, 1, 2)], axis=1)
        return jnp.dot(wide, dense[w, j], preferred_element_type=jnp.float32).astype(jnp.bfloat16)

    def finish(n, rows):
        w, j = n // 4, n % 4
        lanes = slice(256 * j, 256 * j + 256)
        blurred = jnp.dot(mixes[w][0], rows, preferred_element_type=jnp.float32)
        blurred = blurred + jnp.dot(mixes[w][1], rows, preferred_element_type=jnp.float32)
        done[w, :, lanes] = observed[w, :, lanes] / blurred
        copies.append(pltpu.make_async_copy(done.at[w, :, lanes], ratio.at[w, :, lanes], sems.at[n]))
        copies[-1].start()

    rows = lateral(0)
    for n in range(8):
        if n == 0:
            build(1)
        after = lateral(n + 1) if n < 7 else None
        finish(n, rows)
        rows = after
    for copy in copies:
        copy.wait()


def early(z):
    return z < AHEAD


def permute(array, route, chosen=lambda z: True):
    pairs = []
    for z, x, core, v, gy in itertools.product(*map(range, SIZES)):
        if chosen(z):
            to, across = route(v, gy)
            base = ((z * SIZES[1] + x) * SIZES[2] + core) * SIZES[3]
            pairs.append(((base + v) * SIZES[4] + gy, (base + to) * SIZES[4] + across))
    return lax.ppermute(array, AXES, pairs)


def mirror(v, gy):
    return 3 - v, 1 - gy


def shards(estimate, observed, psf_blocks, kernel_y, block_source, psf_columns):
    side = lax.axis_index("gy")
    place = [lax.axis_index("view"), side, lax.axis_index("core"), early(lax.axis_index("z"))]
    place = jnp.stack([jnp.asarray(entry, jnp.int32) for entry in place])
    shard = psf_blocks.reshape(2, 32, 64).transpose(1, 0, 2).reshape(1, 32, 128)
    spread = jnp.broadcast_to(shard, (12, 32, 128))
    begin = jnp.where(side == 0, ROWS - HALO, 0)
    ahead = lax.dynamic_slice_in_dim(estimate, begin, HALO, 1)
    ahead, spread, estimate = lax.optimization_barrier((ahead, spread, estimate))
    ahead = permute(ahead, mirror, early)
    ahead, block_source, psf_columns = lax.optimization_barrier((ahead, block_source, psf_columns))
    first = 2 * lax.axis_index("view")
    numbers = jnp.concatenate([block_source, psf_columns.reshape(8, 48)], axis=1)
    numbers = lax.dynamic_slice_in_dim(numbers, first, 2, 0)
    along = lax.all_to_all(spread, "z", 0, 0, tiled=True)
    slab = jnp.concatenate([estimate.reshape(OWN, 2, 128), ahead.reshape(EDGE, 2, 128)], axis=0)
    slab = slab.transpose(1, 0, 2)
    two = permute(slab, lambda v, gy: (v ^ 2, gy))
    three = permute(slab, lambda v, gy: (v ^ 3, gy))
    late = permute(slab, lambda v, gy: (v ^ 1, gy), lambda z: not early(z))
    rows = [part.reshape(2, 18, 8, 128) for part in (slab, late, two, three)]
    upper = jnp.stack([part[:, 0:16:4, :HALO] for part in rows])
    lower = jnp.stack([part[:, 3:16:4, HALO:] for part in rows])
    rows = jnp.where(side == 0, lower, upper)
    along, rows, slab, numbers = lax.optimization_barrier((along, rows, slab, numbers))
    mine = lax.all_to_all(jnp.broadcast_to(along[None], (4, 12, 32, 128)), "x", 0, 0, tiled=True)
    one = permute(slab, lambda v, gy: (v ^ 1, gy), early)
    edge = permute(rows, mirror, lambda z: not early(z)).reshape(4, 2, EDGE, 128)
    mine, one, edge, kernel_y = lax.optimization_barrier((mine, one, edge, kernel_y))
    mine = mine.reshape(48, 32, 128)
    weights = lax.dynamic_slice_in_dim(kernel_y, first, 2, 0)
    other = lax.ppermute(mine, "core", [(0, 1), (1, 0)])
    smem = pl.BlockSpec(memory_space=pltpu.SMEM)
    vmem = pl.BlockSpec(memory_space=pltpu.VMEM)
    ratio = pl.pallas_call(
        fused,
        out_shape=jax.ShapeDtypeStruct((2, OWN, 1024), jnp.float32),
        in_specs=[smem] * 3 + [vmem] * 9,
        out_specs=pl.BlockSpec(memory_space=pl.ANY),
        scratch_shapes=[
            pltpu.VMEM((2, BLOCKS // 2, 512, 256), jnp.bfloat16),
            pltpu.VMEM((4, 2, OWN + EDGE, 128), jnp.bfloat16),
            pltpu.VMEM((2, OWN, 1024), jnp.float32),
            pltpu.SemaphoreType.DMA((8,)),
        ],
        compiler_params=pltpu.CompilerParams(vmem_limit_bytes=16 * 1024 * 1024),
    )(
        place,
        numbers,
        weights,
        slab,
        one,
        late,
        two,
        three,
        edge,
        mine,
        other,
        observed.reshape(2, OWN, 1024),
    )
    return ratio.reshape(2, PLANES, ROWS, 1024)


def solution(mesh):
    fine = Mesh(mesh.devices.reshape(SIZES), AXES)
    gz = ("z", "x", "core")
    in_specs = (P(gz, "gy", "view"), P("view", gz, "gy", None), P("view", gz), P(), P(), P())
    out_specs = P("view", gz, "gy", None)
    return jax.shard_map(shards, mesh=fine, in_specs=in_specs, out_specs=out_specs, check_vma=False)
```

```python
import itertools

import jax
import jax.numpy as jnp
from jax import lax
from jax.experimental import pallas as pl
from jax.experimental.pallas import tpu as pltpu
from jax.sharding import Mesh, PartitionSpec as P

PLANES, ROWS, HALO = 4, 32, 4
OWN = PLANES * ROWS
EDGE = PLANES * HALO
BLOCKS = 8
BAND = 3
AHEAD = 5
AXES = ("z", "x", "core", "view", "gy")
SIZES = (12, 4, 2, 4, 2)


def fused(place, numbers, weights, own, one, late, two, three, edge, mine, other, observed, ratio, dense, seen, done, sems):
    view, side, core = place[0], place[1], place[2]
    soon = place[3] == 1
    for k, part in enumerate((own[...], jnp.where(soon, one[...], late[...]), two[...], three[...])):
        seen[view ^ k, :, :OWN] = part[:, :OWN]
        seen[view ^ k ^ 3, :, OWN:] = jnp.where(soon, part[:, OWN:], edge[k])

    def build(w):
        dense[w] = jnp.zeros_like(dense[w])
        for i in range(2 * BLOCKS):
            j, quarter = i // 4, i % 4
            for k in range(BAND):
                shift = (numbers[w, BLOCKS + i * BAND + k] - (4 * j - 2)) & 15
                base = shift * 64
                lanes = pl.ds(64 * quarter, 64)
                q = i * BAND + k
                s = q % 4 * 12 + q // 4
                dense[w, j, pl.ds(pl.multiple_of(base + 32 * core, 32), 32), lanes] = mine[
                    s, :, 64 * w : 64 * w + 64
                ]
                dense[w, j, pl.ds(pl.multiple_of(base + 32 * (1 - core), 32), 32), lanes] = other[
                    s, :, 64 * w : 64 * w + 64
                ]

    build(0)

    def block(w, j):
        b = numbers[w, j % BLOCKS]
        return seen[b // 2, b % 2]

    shape = (OWN, OWN + EDGE)
    row = lax.broadcasted_iota(jnp.int32, shape, 0)
    col = lax.broadcasted_iota(jnp.int32, shape, 1)
    outer = col - OWN
    spot = jnp.where(col < OWN, col & (ROWS - 1), (outer & (HALO - 1)) + jnp.where(side == 0, ROWS, -HALO))
    plane = jnp.where(col < OWN, col >> 5, outer >> 2)
    tap = jnp.where(plane == (row >> 5), spot - (row & (ROWS - 1)) + HALO, -1)
    mixes = []
    for w in range(2):
        mix = jnp.zeros(shape, jnp.float32)
        for t in range(2 * HALO + 1):
            mix = jnp.where(tap == t, weights[w, t], mix)
        high = mix.astype(jnp.bfloat16)
        low = (mix - high.astype(jnp.float32)).astype(jnp.bfloat16)
        mixes.append((high, low))

    copies = []

    def lateral(n):
        w, j = n // 4, n % 4
        wide = jnp.concatenate([block(w, 2 * j + BLOCKS + s) for s in (-1, 0, 1, 2)], axis=1)
        return jnp.dot(wide, dense[w, j], preferred_element_type=jnp.float32).astype(jnp.bfloat16)

    def finish(n, rows):
        w, j = n // 4, n % 4
        lanes = slice(256 * j, 256 * j + 256)
        blurred = jnp.dot(mixes[w][0], rows, preferred_element_type=jnp.float32)
        blurred = blurred + jnp.dot(mixes[w][1], rows, preferred_element_type=jnp.float32)
        done[w, :, lanes] = observed[w, :, lanes] / blurred
        copies.append(pltpu.make_async_copy(done.at[w, :, lanes], ratio.at[w, :, lanes], sems.at[n]))
        copies[-1].start()

    rows = lateral(0)
    for n in range(8):
        if n == 0:
            build(1)
        after = lateral(n + 1) if n < 7 else None
        finish(n, rows)
        rows = after
    for copy in copies:
        copy.wait()


def early(z):
    return z < AHEAD


def permute(array, route, chosen=lambda z: True):
    pairs = []
    for z, x, core, v, gy in itertools.product(*map(range, SIZES)):
        if chosen(z):
            to, across = route(v, gy)
            base = ((z * SIZES[1] + x) * SIZES[2] + core) * SIZES[3]
            pairs.append(((base + v) * SIZES[4] + gy, (base + to) * SIZES[4] + across))
    return lax.ppermute(array, AXES, pairs)


def mirror(v, gy):
    return 3 - v, 1 - gy


def shards(estimate, observed, psf_blocks, kernel_y, block_source, psf_columns):
    side = lax.axis_index("gy")
    place = [lax.axis_index("view"), side, lax.axis_index("core"), early(lax.axis_index("z"))]
    place = jnp.stack([jnp.asarray(entry, jnp.int32) for entry in place])
    shard = psf_blocks.reshape(2, 32, 64).transpose(1, 0, 2).reshape(1, 32, 128)
    spread = jnp.broadcast_to(shard, (12, 32, 128))
    begin = jnp.where(side == 0, ROWS - HALO, 0)
    ahead = lax.dynamic_slice_in_dim(estimate, begin, HALO, 1)
    ahead, spread, estimate = lax.optimization_barrier((ahead, spread, estimate))
    ahead = permute(ahead, mirror, early)
    ahead, block_source, psf_columns = lax.optimization_barrier((ahead, block_source, psf_columns))
    first = 2 * lax.axis_index("view")
    numbers = jnp.concatenate([block_source, psf_columns.reshape(8, 48)], axis=1)
    numbers = lax.dynamic_slice_in_dim(numbers, first, 2, 0)
    along = lax.all_to_all(spread, "z", 0, 0, tiled=True)
    slab = jnp.concatenate([estimate.reshape(OWN, 2, 128), ahead.reshape(EDGE, 2, 128)], axis=0)
    slab = lax.optimization_barrier(slab.transpose(1, 0, 2))
    two = permute(slab, lambda v, gy: (v ^ 2, gy))
    three = permute(slab, lambda v, gy: (v ^ 3, gy))
    late = permute(slab, lambda v, gy: (v ^ 1, gy), lambda z: not early(z))
    rows = [part.reshape(2, 18, 8, 128) for part in (slab, late, two, three)]
    upper = jnp.stack([part[:, 0:16:4, :HALO] for part in rows])
    lower = jnp.stack([part[:, 3:16:4, HALO:] for part in rows])
    rows = jnp.where(side == 0, lower, upper)
    along, rows, slab, numbers = lax.optimization_barrier((along, rows, slab, numbers))
    mine = lax.all_to_all(jnp.broadcast_to(along[None], (4, 12, 32, 128)), "x", 0, 0, tiled=True)
    one = permute(slab, lambda v, gy: (v ^ 1, gy), early)
    edge = permute(rows, mirror, lambda z: not early(z)).reshape(4, 2, EDGE, 128)
    mine, one, edge, kernel_y = lax.optimization_barrier((mine, one, edge, kernel_y))
    mine = mine.reshape(48, 32, 128)
    weights = lax.dynamic_slice_in_dim(kernel_y, first, 2, 0)
    other = lax.ppermute(mine, "core", [(0, 1), (1, 0)])
    smem = pl.BlockSpec(memory_space=pltpu.SMEM)
    vmem = pl.BlockSpec(memory_space=pltpu.VMEM)
    ratio = pl.pallas_call(
        fused,
        out_shape=jax.ShapeDtypeStruct((2, OWN, 1024), jnp.float32),
        in_specs=[smem] * 3 + [vmem] * 9,
        out_specs=pl.BlockSpec(memory_space=pl.ANY),
        scratch_shapes=[
            pltpu.VMEM((2, BLOCKS // 2, 512, 256), jnp.bfloat16),
            pltpu.VMEM((4, 2, OWN + EDGE, 128), jnp.bfloat16),
            pltpu.VMEM((2, OWN, 1024), jnp.float32),
            pltpu.SemaphoreType.DMA((8,)),
        ],
        compiler_params=pltpu.CompilerParams(vmem_limit_bytes=16 * 1024 * 1024),
    )(
        place,
        numbers,
        weights,
        slab,
        one,
        late,
        two,
        three,
        edge,
        mine,
        other,
        observed.reshape(2, OWN, 1024),
    )
    return ratio.reshape(2, PLANES, ROWS, 1024)


def solution(mesh):
    fine = Mesh(mesh.devices.reshape(SIZES), AXES)
    gz = ("z", "x", "core")
    in_specs = (P(gz, "gy", "view"), P("view", gz, "gy", None), P("view", gz), P(), P(), P())
    out_specs = P("view", gz, "gy", None)
    return jax.shard_map(shards, mesh=fine, in_specs=in_specs, out_specs=out_specs, check_vma=False)
```

```python
import itertools

import jax
import jax.numpy as jnp
from jax import lax
from jax.experimental import pallas as pl
from jax.experimental.pallas import tpu as pltpu
from jax.sharding import Mesh, PartitionSpec as P

PLANES, ROWS, HALO = 4, 32, 4
OWN = PLANES * ROWS
EDGE = PLANES * HALO
BLOCKS = 8
BAND = 3
AHEAD = 5
AXES = ("z", "x", "core", "view", "gy")
SIZES = (12, 4, 2, 4, 2)


def fused(place, numbers, weights, own, one, late, two, three, edge, mine, other, observed, ratio, dense, seen, done, sems):
    view, side, core = place[0], place[1], place[2]
    soon = place[3] == 1
    for k, part in enumerate((own[...], jnp.where(soon, one[...], late[...]), two[...], three[...])):
        seen[view ^ k, :, :OWN] = part[:, :OWN]
        seen[view ^ k ^ 3, :, OWN:] = jnp.where(soon, part[:, OWN:], edge[k])

    def build(n):
        w, j = n // 4, n % 4
        dense[w, j] = jnp.zeros_like(dense[w, j])
        for quarter in range(4):
            i = 4 * j + quarter
            lanes = pl.ds(64 * quarter, 64)
            for k in range(BAND):
                base = 64 * ((numbers[w, BLOCKS + i * BAND + k] - (4 * j - 2)) & 15)
                q = i * BAND + k
                s = q % 4 * 12 + q // 4
                for half, rows in ((core, mine), (1 - core, other)):
                    at = pl.ds(pl.multiple_of(base + 32 * half, 32), 32)
                    dense[w, j, at, lanes] = rows[s, :, 64 * w : 64 * w + 64]

    build(0)

    def block(w, j):
        b = numbers[w, j % BLOCKS]
        return seen[b // 2, b % 2]

    shape = (OWN, OWN + EDGE)
    row = lax.broadcasted_iota(jnp.int32, shape, 0)
    col = lax.broadcasted_iota(jnp.int32, shape, 1)
    outer = col - OWN
    spot = jnp.where(col < OWN, col & (ROWS - 1), (outer & (HALO - 1)) + jnp.where(side == 0, ROWS, -HALO))
    plane = jnp.where(col < OWN, col >> 5, outer >> 2)
    tap = jnp.where(plane == (row >> 5), spot - (row & (ROWS - 1)) + HALO, -1)
    mixes = []
    for w in range(2):
        mix = jnp.zeros(shape, jnp.float32)
        for t in range(2 * HALO + 1):
            mix = jnp.where(tap == t, weights[w, t], mix)
        high = mix.astype(jnp.bfloat16)
        low = (mix - high.astype(jnp.float32)).astype(jnp.bfloat16)
        mixes.append((high, low))

    copies = []

    def lateral(n):
        w, j = n // 4, n % 4
        wide = jnp.concatenate([block(w, 2 * j + BLOCKS + s) for s in (-1, 0, 1, 2)], axis=1)
        return jnp.dot(wide, dense[w, j], preferred_element_type=jnp.float32).astype(jnp.bfloat16)

    def finish(n, rows):
        w, j = n // 4, n % 4
        lanes = slice(256 * j, 256 * j + 256)
        blurred = jnp.dot(mixes[w][0], rows, preferred_element_type=jnp.float32)
        blurred = blurred + jnp.dot(mixes[w][1], rows, preferred_element_type=jnp.float32)
        done[w, :, lanes] = observed[w, :, lanes] / blurred
        copies.append(pltpu.make_async_copy(done.at[w, :, lanes], ratio.at[w, :, lanes], sems.at[n]))
        copies[-1].start()

    rows = lateral(0)
    for n in range(8):
        if n < 7:
            build(n + 1)
        after = lateral(n + 1) if n < 7 else None
        finish(n, rows)
        rows = after
    for copy in copies:
        copy.wait()


def early(z):
    return z < AHEAD


def permute(array, route, chosen=lambda z: True):
    pairs = []
    for z, x, core, v, gy in itertools.product(*map(range, SIZES)):
        if chosen(z):
            to, across = route(v, gy)
            base = ((z * SIZES[1] + x) * SIZES[2] + core) * SIZES[3]
            pairs.append(((base + v) * SIZES[4] + gy, (base + to) * SIZES[4] + across))
    return lax.ppermute(array, AXES, pairs)


def mirror(v, gy):
    return 3 - v, 1 - gy


def shards(estimate, observed, psf_blocks, kernel_y, block_source, psf_columns):
    side = lax.axis_index("gy")
    place = [lax.axis_index("view"), side, lax.axis_index("core"), early(lax.axis_index("z"))]
    place = jnp.stack([jnp.asarray(entry, jnp.int32) for entry in place])
    shard = psf_blocks.reshape(2, 32, 64).transpose(1, 0, 2).reshape(1, 32, 128)
    spread = jnp.broadcast_to(shard, (12, 32, 128))
    begin = jnp.where(side == 0, ROWS - HALO, 0)
    ahead = lax.dynamic_slice_in_dim(estimate, begin, HALO, 1)
    ahead, spread, estimate = lax.optimization_barrier((ahead, spread, estimate))
    ahead = permute(ahead, mirror, early)
    ahead, block_source, psf_columns = lax.optimization_barrier((ahead, block_source, psf_columns))
    first = 2 * lax.axis_index("view")
    numbers = jnp.concatenate([block_source, psf_columns.reshape(8, 48)], axis=1)
    numbers = lax.dynamic_slice_in_dim(numbers, first, 2, 0)
    along = lax.all_to_all(spread, "z", 0, 0, tiled=True)
    slab = jnp.concatenate([estimate.reshape(OWN, 2, 128), ahead.reshape(EDGE, 2, 128)], axis=0)
    slab = lax.optimization_barrier(slab.transpose(1, 0, 2))
    two = permute(slab, lambda v, gy: (v ^ 2, gy))
    three = permute(slab, lambda v, gy: (v ^ 3, gy))
    late = permute(slab, lambda v, gy: (v ^ 1, gy), lambda z: not early(z))
    rows = [part.reshape(2, 18, 8, 128) for part in (slab, late, two, three)]
    upper = jnp.stack([part[:, 0:16:4, :HALO] for part in rows])
    lower = jnp.stack([part[:, 3:16:4, HALO:] for part in rows])
    rows = jnp.where(side == 0, lower, upper)
    along, rows, slab, numbers = lax.optimization_barrier((along, rows, slab, numbers))
    mine = lax.all_to_all(jnp.broadcast_to(along[None], (4, 12, 32, 128)), "x", 0, 0, tiled=True)
    one = permute(slab, lambda v, gy: (v ^ 1, gy), early)
    edge = permute(rows, mirror, lambda z: not early(z)).reshape(4, 2, EDGE, 128)
    mine, one, edge, kernel_y = lax.optimization_barrier((mine, one, edge, kernel_y))
    mine = mine.reshape(48, 32, 128)
    weights = lax.dynamic_slice_in_dim(kernel_y, first, 2, 0)
    other = lax.ppermute(mine, "core", [(0, 1), (1, 0)])
    smem = pl.BlockSpec(memory_space=pltpu.SMEM)
    vmem = pl.BlockSpec(memory_space=pltpu.VMEM)
    ratio = pl.pallas_call(
        fused,
        out_shape=jax.ShapeDtypeStruct((2, OWN, 1024), jnp.float32),
        in_specs=[smem] * 3 + [vmem] * 9,
        out_specs=pl.BlockSpec(memory_space=pl.ANY),
        scratch_shapes=[
            pltpu.VMEM((2, BLOCKS // 2, 512, 256), jnp.bfloat16),
            pltpu.VMEM((4, 2, OWN + EDGE, 128), jnp.bfloat16),
            pltpu.VMEM((2, OWN, 1024), jnp.float32),
            pltpu.SemaphoreType.DMA((8,)),
        ],
        compiler_params=pltpu.CompilerParams(vmem_limit_bytes=16 * 1024 * 1024),
    )(
        place,
        numbers,
        weights,
        slab,
        one,
        late,
        two,
        three,
        edge,
        mine,
        other,
        observed.reshape(2, OWN, 1024),
    )
    return ratio.reshape(2, PLANES, ROWS, 1024)


def solution(mesh):
    fine = Mesh(mesh.devices.reshape(SIZES), AXES)
    gz = ("z", "x", "core")
    in_specs = (P(gz, "gy", "view"), P("view", gz, "gy", None), P("view", gz), P(), P(), P())
    out_specs = P("view", gz, "gy", None)
    return jax.shard_map(shards, mesh=fine, in_specs=in_specs, out_specs=out_specs, check_vma=False)
```

```python
import itertools

import jax
import jax.numpy as jnp
from jax import lax
from jax.experimental import pallas as pl
from jax.experimental.pallas import tpu as pltpu
from jax.sharding import Mesh, PartitionSpec as P

PLANES, ROWS, HALO = 4, 32, 4
OWN = PLANES * ROWS
EDGE = PLANES * HALO
BLOCKS = 8
BAND = 3
AHEAD = 4
AXES = ("z", "x", "core", "view", "gy")
SIZES = (12, 4, 2, 4, 2)


def fused(place, numbers, weights, own, one, late, two, three, edge, mine, other, observed, ratio, dense, seen, done, sems):
    view, side, core = place[0], place[1], place[2]
    soon = place[3] == 1
    for k, part in enumerate((own[...], jnp.where(soon, one[...], late[...]), two[...], three[...])):
        seen[view ^ k, :, :OWN] = part[:, :OWN]
        seen[view ^ k ^ 3, :, OWN:] = jnp.where(soon, part[:, OWN:], edge[k])

    def build(n):
        w, j = n // 4, n % 4
        dense[w, j] = jnp.zeros_like(dense[w, j])
        for quarter in range(4):
            i = 4 * j + quarter
            lanes = pl.ds(64 * quarter, 64)
            for k in range(BAND):
                base = 64 * ((numbers[w, BLOCKS + i * BAND + k] - (4 * j - 2)) & 15)
                q = i * BAND + k
                s = q % 4 * 12 + q // 4
                for half, rows in ((core, mine), (1 - core, other)):
                    at = pl.ds(pl.multiple_of(base + 32 * half, 32), 32)
                    dense[w, j, at, lanes] = rows[s, :, 64 * w : 64 * w + 64]

    build(0)

    def block(w, j):
        b = numbers[w, j % BLOCKS]
        return seen[b // 2, b % 2]

    shape = (OWN, OWN + EDGE)
    row = lax.broadcasted_iota(jnp.int32, shape, 0)
    col = lax.broadcasted_iota(jnp.int32, shape, 1)
    outer = col - OWN
    spot = jnp.where(col < OWN, col & (ROWS - 1), (outer & (HALO - 1)) + jnp.where(side == 0, ROWS, -HALO))
    plane = jnp.where(col < OWN, col >> 5, outer >> 2)
    tap = jnp.where(plane == (row >> 5), spot - (row & (ROWS - 1)) + HALO, -1)
    mixes = []
    for w in range(2):
        mix = jnp.zeros(shape, jnp.float32)
        for t in range(2 * HALO + 1):
            mix = jnp.where(tap == t, weights[w, t], mix)
        high = mix.astype(jnp.bfloat16)
        low = (mix - high.astype(jnp.float32)).astype(jnp.bfloat16)
        mixes.append((high, low))

    copies = []

    def lateral(n):
        w, j = n // 4, n % 4
        wide = jnp.concatenate([block(w, 2 * j + BLOCKS + s) for s in (-1, 0, 1, 2)], axis=1)
        return jnp.dot(wide, dense[w, j], preferred_element_type=jnp.float32).astype(jnp.bfloat16)

    def finish(n, rows):
        w, j = n // 4, n % 4
        lanes = slice(256 * j, 256 * j + 256)
        blurred = jnp.dot(mixes[w][0], rows, preferred_element_type=jnp.float32)
        blurred = blurred + jnp.dot(mixes[w][1], rows, preferred_element_type=jnp.float32)
        done[w, :, lanes] = observed[w, :, lanes] / blurred
        copies.append(pltpu.make_async_copy(done.at[w, :, lanes], ratio.at[w, :, lanes], sems.at[n]))
        copies[-1].start()

    rows = lateral(0)
    for n in range(8):
        if n < 7:
            build(n + 1)
        after = lateral(n + 1) if n < 7 else None
        finish(n, rows)
        rows = after
    for copy in copies:
        copy.wait()


def early(z):
    return z < AHEAD


def permute(array, route, chosen=lambda z: True):
    pairs = []
    for z, x, core, v, gy in itertools.product(*map(range, SIZES)):
        if chosen(z):
            to, across = route(v, gy)
            base = ((z * SIZES[1] + x) * SIZES[2] + core) * SIZES[3]
            pairs.append(((base + v) * SIZES[4] + gy, (base + to) * SIZES[4] + across))
    return lax.ppermute(array, AXES, pairs)


def mirror(v, gy):
    return 3 - v, 1 - gy


def shards(estimate, observed, psf_blocks, kernel_y, block_source, psf_columns):
    side = lax.axis_index("gy")
    place = [lax.axis_index("view"), side, lax.axis_index("core"), early(lax.axis_index("z"))]
    place = jnp.stack([jnp.asarray(entry, jnp.int32) for entry in place])
    shard = psf_blocks.reshape(2, 32, 64).transpose(1, 0, 2).reshape(1, 32, 128)
    spread = jnp.broadcast_to(shard, (12, 32, 128))
    begin = jnp.where(side == 0, ROWS - HALO, 0)
    ahead = lax.dynamic_slice_in_dim(estimate, begin, HALO, 1)
    ahead, spread, estimate = lax.optimization_barrier((ahead, spread, estimate))
    ahead = permute(ahead, mirror, early)
    ahead, block_source, psf_columns = lax.optimization_barrier((ahead, block_source, psf_columns))
    first = 2 * lax.axis_index("view")
    numbers = jnp.concatenate([block_source, psf_columns.reshape(8, 48)], axis=1)
    numbers = lax.dynamic_slice_in_dim(numbers, first, 2, 0)
    along = lax.all_to_all(spread, "z", 0, 0, tiled=True)
    slab = jnp.concatenate([estimate.reshape(OWN, 2, 128), ahead.reshape(EDGE, 2, 128)], axis=0)
    slab = lax.optimization_barrier(slab.transpose(1, 0, 2))
    two = permute(slab, lambda v, gy: (v ^ 2, gy))
    three = permute(slab, lambda v, gy: (v ^ 3, gy))
    late = permute(slab, lambda v, gy: (v ^ 1, gy), lambda z: not early(z))
    rows = [part.reshape(2, 18, 8, 128) for part in (slab, late, two, three)]
    upper = jnp.stack([part[:, 0:16:4, :HALO] for part in rows])
    lower = jnp.stack([part[:, 3:16:4, HALO:] for part in rows])
    rows = jnp.where(side == 0, lower, upper)
    along, rows, slab, numbers = lax.optimization_barrier((along, rows, slab, numbers))
    mine = lax.all_to_all(jnp.broadcast_to(along[None], (4, 12, 32, 128)), "x", 0, 0, tiled=True)
    one = permute(slab, lambda v, gy: (v ^ 1, gy), early)
    edge = permute(rows, mirror, lambda z: not early(z)).reshape(4, 2, EDGE, 128)
    mine, one, edge, kernel_y = lax.optimization_barrier((mine, one, edge, kernel_y))
    mine = mine.reshape(48, 32, 128)
    weights = lax.dynamic_slice_in_dim(kernel_y, first, 2, 0)
    other = lax.ppermute(mine, "core", [(0, 1), (1, 0)])
    smem = pl.BlockSpec(memory_space=pltpu.SMEM)
    vmem = pl.BlockSpec(memory_space=pltpu.VMEM)
    ratio = pl.pallas_call(
        fused,
        out_shape=jax.ShapeDtypeStruct((2, OWN, 1024), jnp.float32),
        in_specs=[smem] * 3 + [vmem] * 9,
        out_specs=pl.BlockSpec(memory_space=pl.ANY),
        scratch_shapes=[
            pltpu.VMEM((2, BLOCKS // 2, 512, 256), jnp.bfloat16),
            pltpu.VMEM((4, 2, OWN + EDGE, 128), jnp.bfloat16),
            pltpu.VMEM((2, OWN, 1024), jnp.float32),
            pltpu.SemaphoreType.DMA((8,)),
        ],
        compiler_params=pltpu.CompilerParams(vmem_limit_bytes=16 * 1024 * 1024),
    )(
        place,
        numbers,
        weights,
        slab,
        one,
        late,
        two,
        three,
        edge,
        mine,
        other,
        observed.reshape(2, OWN, 1024),
    )
    return ratio.reshape(2, PLANES, ROWS, 1024)


def solution(mesh):
    fine = Mesh(mesh.devices.reshape(SIZES), AXES)
    gz = ("z", "x", "core")
    in_specs = (P(gz, "gy", "view"), P("view", gz, "gy", None), P("view", gz), P(), P(), P())
    out_specs = P("view", gz, "gy", None)
    return jax.shard_map(shards, mesh=fine, in_specs=in_specs, out_specs=out_specs, check_vma=False)
```

```python
import itertools

import jax
import jax.numpy as jnp
from jax import lax
from jax.experimental import pallas as pl
from jax.experimental.pallas import tpu as pltpu
from jax.sharding import Mesh, PartitionSpec as P

PLANES, ROWS, HALO = 4, 32, 4
OWN = PLANES * ROWS
EDGE = PLANES * HALO
BLOCKS = 8
BAND = 3
AHEAD = 3
AXES = ("z", "x", "core", "view", "gy")
SIZES = (12, 4, 2, 4, 2)


def fused(place, numbers, weights, own, one, late, two, three, edge, mine, other, observed, ratio, dense, seen, done, sems):
    view, side, core = place[0], place[1], place[2]
    soon = place[3] == 1
    for k, part in enumerate((own[...], jnp.where(soon, one[...], late[...]), two[...], three[...])):
        seen[view ^ k, :, :OWN] = part[:, :OWN]
        seen[view ^ k ^ 3, :, OWN:] = jnp.where(soon, part[:, OWN:], edge[k])

    def build(n):
        w, j = n // 4, n % 4
        dense[w, j] = jnp.zeros_like(dense[w, j])
        for quarter in range(4):
            i = 4 * j + quarter
            lanes = pl.ds(64 * quarter, 64)
            for k in range(BAND):
                base = 64 * ((numbers[w, BLOCKS + i * BAND + k] - (4 * j - 2)) & 15)
                q = i * BAND + k
                s = q % 4 * 12 + q // 4
                for half, rows in ((core, mine), (1 - core, other)):
                    at = pl.ds(pl.multiple_of(base + 32 * half, 32), 32)
                    dense[w, j, at, lanes] = rows[s, :, 64 * w : 64 * w + 64]

    build(0)

    def block(w, j):
        b = numbers[w, j % BLOCKS]
        return seen[b // 2, b % 2]

    shape = (OWN, OWN + EDGE)
    row = lax.broadcasted_iota(jnp.int32, shape, 0)
    col = lax.broadcasted_iota(jnp.int32, shape, 1)
    outer = col - OWN
    spot = jnp.where(col < OWN, col & (ROWS - 1), (outer & (HALO - 1)) + jnp.where(side == 0, ROWS, -HALO))
    plane = jnp.where(col < OWN, col >> 5, outer >> 2)
    tap = jnp.where(plane == (row >> 5), spot - (row & (ROWS - 1)) + HALO, -1)
    mixes = []
    for w in range(2):
        mix = jnp.zeros(shape, jnp.float32)
        for t in range(2 * HALO + 1):
            mix = jnp.where(tap == t, weights[w, t], mix)
        high = mix.astype(jnp.bfloat16)
        low = (mix - high.astype(jnp.float32)).astype(jnp.bfloat16)
        mixes.append((high, low))

    copies = []

    def lateral(n):
        w, j = n // 4, n % 4
        wide = jnp.concatenate([block(w, 2 * j + BLOCKS + s) for s in (-1, 0, 1, 2)], axis=1)
        return jnp.dot(wide, dense[w, j], preferred_element_type=jnp.float32).astype(jnp.bfloat16)

    def finish(n, rows):
        w, j = n // 4, n % 4
        lanes = slice(256 * j, 256 * j + 256)
        blurred = jnp.dot(mixes[w][0], rows, preferred_element_type=jnp.float32)
        blurred = blurred + jnp.dot(mixes[w][1], rows, preferred_element_type=jnp.float32)
        done[w, :, lanes] = observed[w, :, lanes] / blurred
        copies.append(pltpu.make_async_copy(done.at[w, :, lanes], ratio.at[w, :, lanes], sems.at[n]))
        copies[-1].start()

    rows = lateral(0)
    for n in range(8):
        if n < 7:
            build(n + 1)
        after = lateral(n + 1) if n < 7 else None
        finish(n, rows)
        rows = after
    for copy in copies:
        copy.wait()


def early(z):
    return z < AHEAD


def permute(array, route, chosen=lambda z: True):
    pairs = []
    for z, x, core, v, gy in itertools.product(*map(range, SIZES)):
        if chosen(z):
            to, across = route(v, gy)
            base = ((z * SIZES[1] + x) * SIZES[2] + core) * SIZES[3]
            pairs.append(((base + v) * SIZES[4] + gy, (base + to) * SIZES[4] + across))
    return lax.ppermute(array, AXES, pairs)


def mirror(v, gy):
    return 3 - v, 1 - gy


def shards(estimate, observed, psf_blocks, kernel_y, block_source, psf_columns):
    side = lax.axis_index("gy")
    place = [lax.axis_index("view"), side, lax.axis_index("core"), early(lax.axis_index("z"))]
    place = jnp.stack([jnp.asarray(entry, jnp.int32) for entry in place])
    shard = psf_blocks.reshape(2, 32, 64).transpose(1, 0, 2).reshape(1, 32, 128)
    spread = jnp.broadcast_to(shard, (12, 32, 128))
    begin = jnp.where(side == 0, ROWS - HALO, 0)
    ahead = lax.dynamic_slice_in_dim(estimate, begin, HALO, 1)
    ahead, spread, estimate = lax.optimization_barrier((ahead, spread, estimate))
    ahead = permute(ahead, mirror, early)
    ahead, block_source, psf_columns = lax.optimization_barrier((ahead, block_source, psf_columns))
    first = 2 * lax.axis_index("view")
    numbers = jnp.concatenate([block_source, psf_columns.reshape(8, 48)], axis=1)
    numbers = lax.dynamic_slice_in_dim(numbers, first, 2, 0)
    along = lax.all_to_all(spread, "z", 0, 0, tiled=True)
    slab = jnp.concatenate([estimate.reshape(OWN, 2, 128), ahead.reshape(EDGE, 2, 128)], axis=0)
    slab = lax.optimization_barrier(slab.transpose(1, 0, 2))
    two = permute(slab, lambda v, gy: (v ^ 2, gy))
    three = permute(slab, lambda v, gy: (v ^ 3, gy))
    late = permute(slab, lambda v, gy: (v ^ 1, gy), lambda z: not early(z))
    rows = [part.reshape(2, 18, 8, 128) for part in (slab, late, two, three)]
    upper = jnp.stack([part[:, 0:16:4, :HALO] for part in rows])
    lower = jnp.stack([part[:, 3:16:4, HALO:] for part in rows])
    rows = jnp.where(side == 0, lower, upper)
    along, rows, slab, numbers = lax.optimization_barrier((along, rows, slab, numbers))
    mine = lax.all_to_all(jnp.broadcast_to(along[None], (4, 12, 32, 128)), "x", 0, 0, tiled=True)
    one = permute(slab, lambda v, gy: (v ^ 1, gy), early)
    edge = permute(rows, mirror, lambda z: not early(z)).reshape(4, 2, EDGE, 128)
    mine, one, edge, kernel_y = lax.optimization_barrier((mine, one, edge, kernel_y))
    mine = mine.reshape(48, 32, 128)
    weights = lax.dynamic_slice_in_dim(kernel_y, first, 2, 0)
    other = lax.ppermute(mine, "core", [(0, 1), (1, 0)])
    smem = pl.BlockSpec(memory_space=pltpu.SMEM)
    vmem = pl.BlockSpec(memory_space=pltpu.VMEM)
    ratio = pl.pallas_call(
        fused,
        out_shape=jax.ShapeDtypeStruct((2, OWN, 1024), jnp.float32),
        in_specs=[smem] * 3 + [vmem] * 9,
        out_specs=pl.BlockSpec(memory_space=pl.ANY),
        scratch_shapes=[
            pltpu.VMEM((2, BLOCKS // 2, 512, 256), jnp.bfloat16),
            pltpu.VMEM((4, 2, OWN + EDGE, 128), jnp.bfloat16),
            pltpu.VMEM((2, OWN, 1024), jnp.float32),
            pltpu.SemaphoreType.DMA((8,)),
        ],
        compiler_params=pltpu.CompilerParams(vmem_limit_bytes=16 * 1024 * 1024),
    )(
        place,
        numbers,
        weights,
        slab,
        one,
        late,
        two,
        three,
        edge,
        mine,
        other,
        observed.reshape(2, OWN, 1024),
    )
    return ratio.reshape(2, PLANES, ROWS, 1024)


def solution(mesh):
    fine = Mesh(mesh.devices.reshape(SIZES), AXES)
    gz = ("z", "x", "core")
    in_specs = (P(gz, "gy", "view"), P("view", gz, "gy", None), P("view", gz), P(), P(), P())
    out_specs = P("view", gz, "gy", None)
    return jax.shard_map(shards, mesh=fine, in_specs=in_specs, out_specs=out_specs, check_vma=False)
```
